32 devices in a mesh: row: 16 (over z, y, x), col: 2 (over core).
Axes of the slice: x: 2, y: 2, z: 4, core: 2. Of those that a mesh axis runs over, the one named last changes fastest.
Arguments:
- a_tiles: bfloat16 [256, 7, 4096], P('row'), may hold values from -0.25 to 0.25
- neighbors: int32 [256, 7], P('row'), may hold values from 0 to 143, as said below
- send_rows: int32 [16, 128], P('row'), may hold values from 0 to 15
- p_tiles: bfloat16 [256, 2, 4096], P('row', 'col'), may hold values from -0.75 to 0.75
- p_index: int32 [256, 2], P('row', 'col'), may hold values from 0 to 1
Outputs:
- coarse: float32 [256, 256], P('row', 'col')
The draws below stay inside these ranges and needn't reach their ends.
Inputs may be any that keep to these rules, and one draw needn't show every extreme that they name: `neighbors`: column 0 of a row names the row itself (local index). Other entries below 16 are local rows. An entry v >= 16 names slot s = (v - 16) % 8 filled by device p = (v - 16) // 8, never the reading device itself; s < 8 when p is next to the reader along the row axis (with wrap), s < 4 otherwise.
All inputs are finite; a program needn't handle non-finite values.
Results may differ from the reference program's by a relative error of at most 0.0029.
Values may be sent and summed in bfloat16 or wider, within the bound.
No kernel may reach another device: no remote copies, remote signals or barrier semaphores. Data moves between devices by JAX's collectives and lax.ppermute only.
A program may use at most 64 MiB of HBM per device.

```python
import jax
import jax.numpy as jnp
from jax import lax

B = 64
K = 7
CP = 2
S = 8
S2 = 4
R_DEV = 16
NF = 256
N_ROW = 16
N_COL = 2


def ghost_counts(key):
    far_key = jax.random.fold_in(key, 11)
    source = jnp.arange(N_ROW)[:, None]
    target = jnp.arange(N_ROW)[None, :]
    gap = (target - source) % N_ROW
    far = jax.random.randint(far_key, (N_ROW, N_ROW), max(S2 - 1, 1), S2 + 1)
    near = (gap == 1) | (gap == N_ROW - 1)
    counts = jnp.where(near, S, jnp.where(gap == 2, S2, jnp.where(gap == 0, 0, far)))
    return counts.astype(jnp.int32)


def draw_neighbors(key, part):
    counts = ghost_counts(key)
    pick_key = jax.random.fold_in(key, 37)
    slots = jnp.arange(S, dtype=jnp.int32)
    sources = jnp.arange(N_ROW, dtype=jnp.int32)
    total_codes = N_ROW * S

    def for_device(target):
        gap = (target - sources) % N_ROW
        live = slots[None, :] < counts[:, target][:, None]
        forced = (gap == 1) | (gap == N_ROW - 1) | (gap == 2) | (gap == N_ROW // 2)
        code = R_DEV + sources[:, None] * S + slots[None, :]
        rank = jax.random.permutation(jax.random.fold_in(pick_key, target), total_codes).astype(jnp.int32).reshape(N_ROW, S)
        score = jnp.where(live & forced[:, None], rank, jnp.where(live, rank + total_codes, rank + 2 * total_codes))
        order = jnp.argsort(score.reshape(-1), stable=True)
        total = jnp.sum(live.astype(jnp.int32))
        pick = jnp.arange(R_DEV * 4, dtype=jnp.int32) % total
        return code.reshape(-1)[order[pick]].reshape(R_DEV, 4)
    remote = jax.vmap(for_device)(sources).reshape(N_ROW * R_DEV, 4)
    local_key = jax.random.fold_in(key, 23)
    local = jax.random.randint(local_key, (N_ROW * R_DEV, K - 5), 0, R_DEV)
    itself = (jnp.arange(N_ROW * R_DEV, dtype=jnp.int32) % R_DEV)[:, None]
    return jnp.concatenate([itself, remote, local], axis=1).astype(jnp.int32)


def set_ends(values, stream_key, low, largest):
    longest = values.shape.index(max(values.shape))
    spots = []
    for shift in (0, 1):
        where = [jax.random.randint(jax.random.fold_in(stream_key, axis), (), 0, length) for axis, length in enumerate(values.shape)]
        where[longest] = (where[longest] + shift) % values.shape[longest]
        spots.append(tuple(where))
    return values.at[spots[0]].set(low).at[spots[1]].set(largest)


def block_levels(rng, shape, pieces, least, high):
    level = 1.0
    for dim, parts in pieces:
        heights = jax.random.uniform(jax.random.fold_in(jax.random.fold_in(rng, 6), dim), (parts,), jnp.float32, least / len(pieces), high / len(pieces))
        level = level * jnp.repeat(jnp.exp(heights), shape[dim] // parts).reshape((-1,) + (1,) * (len(shape) - 1 - dim))
    return level


def normal_values(stream_key, shape, deviation, limit, split=(), kind=jnp.bfloat16):
    level = block_levels(stream_key, shape, split, -0.22, 0.18) if split else 1.0
    values = jax.random.normal(stream_key, shape, jnp.float32) * deviation * level
    return jnp.minimum(jnp.maximum(values, -limit), limit).astype(kind)


def setup_inputs(seed: int = 0) -> dict:
    key_of = jax.random.split(jax.random.key(seed), 6)
    a_tiles = normal_values(key_of[0], (NF, K, B * B), (K * B) ** -0.5, 0.25, ((0, 16),))
    neighbors = draw_neighbors(jax.random.fold_in(key_of[5], 71), 0)
    send_rows = set_ends(jax.random.randint(key_of[2], (N_ROW, N_ROW * S), 0, R_DEV), jax.random.fold_in(key_of[2], 1), 0, R_DEV - 1).astype(jnp.int32)
    p_tiles = normal_values(key_of[3], (NF, N_COL, B * B), ((R_DEV * N_ROW * B // (2 * CP)) ** 0.5) ** -0.5, 0.75, ((0, 16), (1, 2)))
    p_index = set_ends(jax.random.randint(key_of[4], (NF, N_COL), 0, CP), jax.random.fold_in(key_of[4], 1), 0, CP - 1).astype(jnp.int32)
    return {"a_tiles": a_tiles, "neighbors": neighbors, "send_rows": send_rows, "p_tiles": p_tiles, "p_index": p_index}


def reference(a_tiles, neighbors, send_rows, p_tiles, p_index):
    panels = p_tiles.shape[1]
    flat_send = send_rows.reshape(-1)
    coarse_blocks = CP * panels

    def device_term(q, total):
        code = lax.dynamic_slice_in_dim(neighbors, q * R_DEV, R_DEV, 0)
        local = code < R_DEV
        ghost = jnp.maximum(code - R_DEV, 0)
        source = ghost // S
        slot = ghost % S
        remote = source * R_DEV + flat_send[source * (N_ROW * S) + q * S + slot]
        glob = jnp.where(local, q * R_DEV + code, remote).astype(jnp.int32)
        tiles = p_tiles[glob].astype(jnp.float32).reshape(R_DEV, K, panels, B, B)
        index = p_index[glob]
        hit = (index[..., None] == jnp.arange(CP)[None, None, None, :]).astype(jnp.float32)
        block_rows = lax.dynamic_slice_in_dim(a_tiles, q * R_DEV, R_DEV, 0)
        coupling = block_rows.astype(jnp.float32).reshape(R_DEV, K, B, B)
        inner = jnp.einsum('rkij,rkcjl->rkcil', coupling, tiles, precision=lax.Precision.HIGHEST)
        product = jnp.einsum('rkcil,rkcb->ricbl', inner, hit, precision=lax.Precision.HIGHEST)
        product = product.astype(jnp.bfloat16).astype(jnp.float32).reshape(R_DEV * B, coarse_blocks * B)
        mine = lax.dynamic_slice_in_dim(p_tiles, q * R_DEV, R_DEV, 0).astype(jnp.float32).reshape(R_DEV, panels, B, B)
        mine_index = lax.dynamic_slice_in_dim(p_index, q * R_DEV, R_DEV, 0)
        mine_hit = (mine_index[..., None] == jnp.arange(CP)[None, None, :]).astype(jnp.float32)
        dense = jnp.einsum('rcix,rcy->ricyx', mine, mine_hit, precision=lax.Precision.HIGHEST)
        dense = dense.reshape(R_DEV * B, coarse_blocks * B)
        return total + jnp.dot(dense.T, product, precision=lax.Precision.HIGHEST, preferred_element_type=jnp.float32)

    start = jnp.zeros((coarse_blocks * B, coarse_blocks * B), jnp.float32)
    return lax.fori_loop(0, N_ROW, device_term, start)
```

```python
import functools

import jax
import jax.numpy as jnp
from jax import lax
from jax.experimental import pallas as pl
from jax.experimental.pallas import tpu as pltpu
from jax.sharding import PartitionSpec as P

B = 64
CP = 2
S = 8
S2 = 4
LANES = 128
PACK = B * B // LANES
BF16 = jnp.bfloat16
VMEM = pl.BlockSpec(memory_space=pltpu.VMEM)
SMEM = pl.BlockSpec(memory_space=pltpu.SMEM)
PARAMS = pltpu.CompilerParams(vmem_limit_bytes=40 * 2**20)


def unpack_rows(flat, scratch):
    for l in range(PACK):
        scratch[:, l, :] = flat[:, l * LANES : (l + 1) * LANES].astype(jnp.float32)


def swap_halves(x):
    return jnp.concatenate([x[:, B:], x[:, :B]], axis=1)


def turn_rows(flat, index_of, scratch, out, base):
    rows = scratch.shape[0]
    unpack_rows(flat, scratch)
    for r in range(rows):
        x = scratch[r]
        x = jnp.where(index_of(r) == 0, x, swap_halves(x))
        out[base + r * PACK : base + (r + 1) * PACK, :] = x.astype(BF16)


def mask_row(index, shape):
    lane = lax.broadcasted_iota(jnp.int32, shape, len(shape) - 1)
    return jnp.where((lane >= B) == (index != 0), 1.0, 0.0)


def widen(x, mask):
    return x * mask, swap_halves(x) * mask


def mask_table(index_of, rows):
    sub = lax.broadcasted_iota(jnp.int32, (rows, LANES), 0)
    table = jnp.zeros((rows, LANES), jnp.float32)
    for r in range(rows):
        table = jnp.where(sub == r, mask_row(index_of(r), (rows, LANES)), table)
    return table


def fill(ref, block, table, picks, marks):
    sub = lax.broadcasted_iota(jnp.int32, (marks, LANES), 0)
    mark = jnp.zeros((marks, LANES), jnp.float32)
    for s, (row, index) in enumerate(picks):
        tile = table[pl.ds(pl.multiple_of(row * PACK, PACK), PACK), :]
        ref[(*block, pl.ds(s * PACK, PACK), slice(None))] = tile
        mark = jnp.where(sub == s, mask_row(index, (marks, LANES)), mark)
    ref[(*block, pl.ds(len(picks) * PACK, marks), slice(None))] = mark.astype(BF16)


def own_kernel(n, send_ref, index_ref, flat_ref, own_ref, left_ref, right_ref, scratch):
    rows = flat_ref.shape[0]
    me = lax.axis_index("row")
    turn_rows(flat_ref, lambda r: index_ref[0, r], scratch, own_ref, 0)
    own_ref[rows * PACK :, :] = mask_table(lambda r: index_ref[0, r], rows).astype(BF16)

    def look(slot):
        row = send_ref[0, slot]
        return row, index_ref[0, row]

    for ref, step in ((left_ref, n - 1), (right_ref, 1)):
        first = lax.rem(me + step, n) * S
        fill(ref, (), own_ref, [look(first + s) for s in range(S2, S)], 8)


def pack_kernel(n, send_ref, index_ref, far_ref, own_ref, flat_ref, out_ref, scratch, table):
    rows = flat_ref.shape[0]
    half = n // 2
    me = lax.axis_index("row")
    base = me - lax.rem(me, half)
    turn_rows(flat_ref, lambda r: far_ref[0, n * S + r], scratch, table, rows * PACK)
    table[: rows * PACK, :] = own_ref[: rows * PACK, :]

    def near_row(slot):
        row = send_ref[0, slot]
        return row, index_ref[0, row]

    def far_row(slot):
        row = far_ref[0, slot]
        return rows + row, far_ref[0, n * S + row]

    for j in range(half):
        first = (base + j) * S
        picks = [near_row(first + s) for s in range(S2)] + [far_row(first + s) for s in range(S2)]
        fill(out_ref, (j,), table, picks, 8)


def coupling_kernel(a_ref, coupling_ref, scratch):
    span, rows, _ = a_ref.shape
    src = lax.broadcasted_iota(jnp.int32, (LANES, LANES), 0)
    dst = lax.broadcasted_iota(jnp.int32, (LANES, LANES), 1)
    part = lax.rem(dst, B)
    want = (dst - part) + jnp.where(part < B // 2, 2 * part, 2 * part - B + 1)
    order = (src == want).astype(BF16)
    for k in range(span):
        unpack_rows(a_ref.at[k], scratch.at[k % 2])
        packed = scratch[k % 2].reshape(rows * PACK, LANES).astype(BF16)
        ordered = jnp.dot(packed, order, preferred_element_type=jnp.float32)
        even = ordered[:, :B].astype(BF16).reshape(rows, PACK, B)
        odd = ordered[:, B:].astype(BF16).reshape(rows, PACK, B)
        coupling_ref[:, :PACK, k * B : (k + 1) * B] = even
        coupling_ref[:, PACK:, k * B : (k + 1) * B] = odd


def restrict_kernel(rows, col_size, *refs):
    panel_refs, restrict_ref = refs[:col_size], refs[col_size]
    mine = lax.axis_index("col")
    for j, panel_ref in enumerate(panel_refs):
        panel = lax.rem(mine + col_size - j, col_size)
        pieces = []
        for r in range(rows):
            mask = panel_ref[rows * PACK + r : rows * PACK + r + 1, :].astype(jnp.float32)
            x = panel_ref[r * PACK : (r + 1) * PACK, :].astype(jnp.float32)
            pieces.extend(widen(x, mask))
        wide = jnp.concatenate(pieces, axis=0)
        restrict_ref[pl.ds(pl.multiple_of(panel * CP * B, LANES), CP * B), :] = wide.T.astype(BF16)


def product_kernel(
    n, code_ref, ghost_ref, left_ref, right_ref, own_ref, coupling_ref, restrict_ref, out_ref, wide, ap
):
    half = n // 2
    rows = coupling_ref.shape[0]
    span = code_ref.shape[0]
    me = lax.axis_index("row")
    base = me - lax.rem(me, half)

    def place(slot, tile, mask):
        even, odd = widen(tile, mask)
        to = pl.multiple_of(slot * B, B)
        wide[pl.ds(to, PACK), :] = even
        wide[pl.ds(pl.multiple_of(to + PACK, PACK), PACK), :] = odd

    def place_slots(first, ref, block, at, marks_at):
        for s in range(S2):
            tile = ref[(*block, pl.ds((at + s) * PACK, PACK), slice(None))]
            place(rows + first + s, tile, ref[(*block, pl.ds(marks_at + at + s, 1), slice(None))])

    for r in range(rows):
        place(r, own_ref[r * PACK : (r + 1) * PACK, :], own_ref[rows * PACK + r : rows * PACK + r + 1, :])
    for j in range(half):
        place_slots((base + j) * S, ghost_ref, (j,), 0, 2 * S2 * PACK)
        place_slots(lax.rem(base + half + j, n) * S, ghost_ref, (j,), S2, 2 * S2 * PACK)
    for ref, step in ((left_ref, n - 1), (right_ref, 1)):
        place_slots(lax.rem(me + step, n) * S + S2, ref, (), 0, S2 * PACK)

    def row_body(r, carry):
        picked = jnp.concatenate(
            [wide[pl.ds(pl.multiple_of(code_ref[k, r] * B, B), B), :] for k in range(span)], axis=0
        )
        block = jnp.dot(coupling_ref[r], picked, preferred_element_type=jnp.float32)
        ap[pl.ds(pl.multiple_of(r * B, B), B), :] = block.astype(BF16)
        return carry

    lax.fori_loop(0, rows, row_body, 0, unroll=8)
    out_ref[...] = jnp.dot(restrict_ref[...], ap[...], preferred_element_type=jnp.float32)


def shards(n, col_size, a_tiles, neighbors, send_rows, p_tiles, p_index):
    rows, span = a_tiles.shape[0], a_tiles.shape[1]
    half = n // 2
    halves = [list(range(half)), list(range(half, n))]
    flat = p_tiles[:, 0, :]
    index = p_index.T
    f32 = jnp.float32

    def call(body, out_shape, scratch_shapes, operands, smem, name, flops=10**7):
        return pl.pallas_call(
            body,
            out_shape=out_shape,
            in_specs=[SMEM] * smem + [VMEM] * (len(operands) - smem),
            out_specs=jax.tree.map(lambda _: VMEM, out_shape),
            scratch_shapes=scratch_shapes,
            compiler_params=PARAMS,
            cost_estimate=pl.CostEstimate(flops=flops, bytes_accessed=2**20, transcendentals=0),
            name=name,
        )(*operands)

    def shape(*dims, dtype=BF16):
        return jax.ShapeDtypeStruct(dims, dtype)

    def ring(x, step):
        return lax.ppermute(x, "row", [(i, (i + step) % n) for i in range(n)])

    unpacked = pltpu.VMEM((rows, PACK, LANES), f32)
    far_flat = ring(flat, half)
    far_ints = ring(jnp.concatenate([send_rows, index], axis=1), half)
    edge = shape(S2 * PACK + 8, LANES)
    own, left, right = call(
        functools.partial(own_kernel, n),
        [shape(rows * PACK + rows, LANES), edge, edge],
        [unpacked],
        (send_rows, index, flat),
        2,
        "own",
    )
    from_right, from_left = ring(left, n - 1), ring(right, 1)
    panels = [own] + [
        lax.ppermute(own, "col", [(i, (i + j) % col_size) for i in range(col_size)])
        for j in range(1, col_size)
    ]
    far_flat, far_ints, from_left, from_right = lax.optimization_barrier(
        (far_flat, far_ints, from_left, from_right)
    )
    out = call(
        functools.partial(pack_kernel, n),
        shape(half, 2 * S2 * PACK + 8, LANES),
        [unpacked, pltpu.VMEM((2 * rows * PACK, LANES), BF16)],
        (send_rows, index, far_ints, own, far_flat),
        3,
        "pack",
    )
    out, a_tiles = lax.optimization_barrier((out, a_tiles))
    ghosts = lax.all_to_all(out, "row", split_axis=0, concat_axis=0, tiled=True, axis_index_groups=halves)
    coupling = call(
        coupling_kernel,
        shape(rows, B, span * B),
        [pltpu.VMEM((2, rows, PACK, LANES), f32)],
        (a_tiles.transpose(1, 0, 2),),
        0,
        "coupling",
        2 * 10**9,
    )
    restrict = call(
        functools.partial(restrict_kernel, rows, col_size),
        shape(col_size * CP * B, rows * B),
        [],
        panels,
        0,
        "restrict",
        2 * 10**8,
    )
    partial = call(
        functools.partial(product_kernel, n),
        shape(col_size * CP * B, CP * B, dtype=f32),
        [pltpu.VMEM(((rows + n * S) * B, LANES), BF16), pltpu.VMEM((rows * B, CP * B), BF16)],
        (neighbors.T, ghosts, from_left, from_right, own, coupling, restrict),
        1,
        "product",
        2 * 10**8,
    )
    share = col_size * CP * B // n
    parts = lax.all_to_all(
        partial.reshape(n, share, CP * B), "row", split_axis=0, concat_axis=0, tiled=True
    )
    return jnp.sum(parts, axis=0)


def solution(mesh):
    in_specs = (
        P("row", None, None),
        P("row", None),
        P("row", None),
        P("row", "col", None),
        P("row", "col"),
    )
    out_specs = P("row", "col")
    body = functools.partial(shards, mesh.shape["row"], mesh.shape["col"])
    return jax.shard_map(body, mesh=mesh, in_specs=in_specs, out_specs=out_specs, check_vma=False)
```

```python
import functools

import jax
import jax.numpy as jnp
from jax import lax
from jax.experimental import pallas as pl
from jax.experimental.pallas import tpu as pltpu
from jax.sharding import PartitionSpec as P

B = 64
CP = 2
S = 8
S2 = 4
LANES = 128
PACK = B * B // LANES
BF16 = jnp.bfloat16
VMEM = pl.BlockSpec(memory_space=pltpu.VMEM)
SMEM = pl.BlockSpec(memory_space=pltpu.SMEM)
PARAMS = pltpu.CompilerParams(vmem_limit_bytes=40 * 2**20)


def unpack_rows(flat, scratch):
    for l in range(PACK):
        scratch[:, l, :] = flat[:, l * LANES : (l + 1) * LANES].astype(jnp.float32)


def swap_halves(x):
    return jnp.concatenate([x[:, B:], x[:, :B]], axis=1)


def turn_rows(flat, index_of, scratch, out, base):
    rows = scratch.shape[0]
    unpack_rows(flat, scratch)
    for r in range(rows):
        x = scratch[r]
        x = jnp.where(index_of(r) == 0, x, swap_halves(x))
        out[base + r * PACK : base + (r + 1) * PACK, :] = x.astype(BF16)


def mask_row(index, shape):
    lane = lax.broadcasted_iota(jnp.int32, shape, len(shape) - 1)
    return jnp.where((lane >= B) == (index != 0), 1.0, 0.0)


def widen(x, mask):
    return x * mask, swap_halves(x) * mask


def mask_table(index_of, rows):
    sub = lax.broadcasted_iota(jnp.int32, (rows, LANES), 0)
    table = jnp.zeros((rows, LANES), jnp.float32)
    for r in range(rows):
        table = jnp.where(sub == r, mask_row(index_of(r), (rows, LANES)), table)
    return table


def fill(ref, block, table, picks, marks):
    sub = lax.broadcasted_iota(jnp.int32, (marks, LANES), 0)
    mark = jnp.zeros((marks, LANES), jnp.float32)
    for s, (row, index) in enumerate(picks):
        tile = table[pl.ds(pl.multiple_of(row * PACK, PACK), PACK), :]
        ref[(*block, pl.ds(s * PACK, PACK), slice(None))] = tile
        mark = jnp.where(sub == s, mask_row(index, (marks, LANES)), mark)
    ref[(*block, pl.ds(len(picks) * PACK, marks), slice(None))] = mark.astype(BF16)


def own_kernel(n, send_ref, index_ref, flat_ref, own_ref, near_ref, left_ref, right_ref, scratch):
    rows = flat_ref.shape[0]
    half = n // 2
    me = lax.axis_index("row")
    base = me - lax.rem(me, half)
    turn_rows(flat_ref, lambda r: index_ref[0, r], scratch, own_ref, 0)
    own_ref[rows * PACK :, :] = mask_table(lambda r: index_ref[0, r], rows).astype(BF16)

    def look(slot):
        row = send_ref[0, slot]
        return row, index_ref[0, row]

    for j in range(half):
        fill(near_ref, (j,), own_ref, [look((base + j) * S + s) for s in range(S2)], 8)
    for ref, step in ((left_ref, n - 1), (right_ref, 1)):
        first = lax.rem(me + step, n) * S
        fill(ref, (), own_ref, [look(first + s) for s in range(S2, S)], 8)


def far_kernel(n, far_ref, flat_ref, out_ref, scratch, table):
    half = n // 2
    me = lax.axis_index("row")
    base = me - lax.rem(me, half)
    turn_rows(flat_ref, lambda r: far_ref[0, n * S + r], scratch, table, 0)

    def look(slot):
        row = far_ref[0, slot]
        return row, far_ref[0, n * S + row]

    for j in range(half):
        fill(out_ref, (j,), table, [look((base + j) * S + s) for s in range(S2)], 8)


def coupling_kernel(a_ref, coupling_ref, scratch):
    span, rows, _ = a_ref.shape
    src = lax.broadcasted_iota(jnp.int32, (2 * LANES, 2 * LANES), 0)
    dst = lax.broadcasted_iota(jnp.int32, (2 * LANES, 2 * LANES), 1)
    odd, block, part = dst // LANES, lax.rem(dst // B, 2), lax.rem(dst, B)
    column = jnp.where(part < B // 2, 2 * part, 2 * part - B + 1)
    order = (src == block * LANES + odd * B + column).astype(BF16)
    for pair in range(pl.cdiv(span, 2)):
        blocks = range(2 * pair, min(2 * pair + 2, span))
        buffer = scratch.at[pair % 2]
        for k in blocks:
            unpack_rows(a_ref.at[k], buffer.at[:, :, pl.ds((k % 2) * LANES, LANES)])
        width = len(blocks) * LANES
        packed = buffer[:, :, :width].reshape(rows * PACK, width).astype(BF16)
        ordered = jnp.dot(packed, order[:width], preferred_element_type=jnp.float32).astype(BF16)
        lanes = pl.ds(pair * LANES, LANES)
        coupling_ref[:, :PACK, lanes] = ordered[:, :LANES].reshape(rows, PACK, LANES)
        coupling_ref[:, PACK:, lanes] = ordered[:, LANES:].reshape(rows, PACK, LANES)


def restrict_kernel(rows, col_size, *refs):
    panel_refs, restrict_ref = refs[:col_size], refs[col_size]
    mine = lax.axis_index("col")
    for j, panel_ref in enumerate(panel_refs):
        panel = lax.rem(mine + col_size - j, col_size)
        pieces = []
        for r in range(rows):
            mask = panel_ref[rows * PACK + r : rows * PACK + r + 1, :].astype(jnp.float32)
            x = panel_ref[r * PACK : (r + 1) * PACK, :].astype(jnp.float32)
            pieces.extend(widen(x, mask))
        wide = jnp.concatenate(pieces, axis=0)
        restrict_ref[pl.ds(pl.multiple_of(panel * CP * B, LANES), CP * B), :] = wide.T.astype(BF16)


def product_kernel(
    n, code_ref, near_ref, far_ref, left_ref, right_ref, own_ref, coupling_ref, restrict_ref, out_ref, wide, ap
):
    half = n // 2
    rows = coupling_ref.shape[0]
    span = code_ref.shape[0]
    me = lax.axis_index("row")
    base = me - lax.rem(me, half)

    def place(slot, tile, mask):
        even, odd = widen(tile, mask)
        to = pl.multiple_of(slot * B, B)
        wide[pl.ds(to, PACK), :] = even
        wide[pl.ds(pl.multiple_of(to + PACK, PACK), PACK), :] = odd

    def place_slots(first, ref, block):
        for s in range(S2):
            tile = ref[(*block, pl.ds(s * PACK, PACK), slice(None))]
            place(rows + first + s, tile, ref[(*block, pl.ds(S2 * PACK + s, 1), slice(None))])

    for r in range(rows):
        place(r, own_ref[r * PACK : (r + 1) * PACK, :], own_ref[rows * PACK + r : rows * PACK + r + 1, :])
    for j in range(half):
        place_slots((base + j) * S, near_ref, (j,))
        place_slots(lax.rem(base + half + j, n) * S, far_ref, (j,))
    for ref, step in ((left_ref, n - 1), (right_ref, 1)):
        place_slots(lax.rem(me + step, n) * S + S2, ref, ())

    def row_body(r, carry):
        picked = jnp.concatenate(
            [wide[pl.ds(pl.multiple_of(code_ref[k, r] * B, B), B), :] for k in range(span)], axis=0
        )
        block = jnp.dot(coupling_ref[r, :, : span * B], picked, preferred_element_type=jnp.float32)
        ap[pl.ds(pl.multiple_of(r * B, B), B), :] = block.astype(BF16)
        return carry

    lax.fori_loop(0, rows, row_body, 0, unroll=8)
    out_ref[...] = jnp.dot(restrict_ref[...], ap[...], preferred_element_type=jnp.float32)


def shards(n, col_size, a_tiles, neighbors, send_rows, p_tiles, p_index):
    rows, span = a_tiles.shape[0], a_tiles.shape[1]
    half = n // 2
    halves = [list(range(half)), list(range(half, n))]
    flat = p_tiles[:, 0, :]
    index = p_index.T
    f32 = jnp.float32

    def call(body, out_shape, scratch_shapes, operands, smem, name, flops=10**7):
        return pl.pallas_call(
            body,
            out_shape=out_shape,
            in_specs=[SMEM] * smem + [VMEM] * (len(operands) - smem),
            out_specs=jax.tree.map(lambda _: VMEM, out_shape),
            scratch_shapes=scratch_shapes,
            compiler_params=PARAMS,
            cost_estimate=pl.CostEstimate(flops=flops, bytes_accessed=2**20, transcendentals=0),
            name=name,
        )(*operands)

    def shape(*dims, dtype=BF16):
        return jax.ShapeDtypeStruct(dims, dtype)

    def exchange(x):
        return lax.all_to_all(x, "row", split_axis=0, concat_axis=0, tiled=True, axis_index_groups=halves)

    def ring(x, step):
        return lax.ppermute(x, "row", [(i, (i + step) % n) for i in range(n)])

    unpacked = pltpu.VMEM((rows, PACK, LANES), f32)
    far_flat = ring(flat, half)
    far_ints = ring(jnp.concatenate([send_rows, index], axis=1), half)
    edge = shape(S2 * PACK + 8, LANES)
    blocks = shape(half, S2 * PACK + 8, LANES)
    own, near, left, right = call(
        functools.partial(own_kernel, n),
        [shape(rows * PACK + rows, LANES), blocks, edge, edge],
        [unpacked],
        (send_rows, index, flat),
        2,
        "own",
    )
    near = exchange(near)
    from_right, from_left = ring(left, n - 1), ring(right, 1)
    panels = [own] + [
        lax.ppermute(own, "col", [(i, (i + j) % col_size) for i in range(col_size)])
        for j in range(1, col_size)
    ]
    far = call(
        functools.partial(far_kernel, n),
        blocks,
        [unpacked, pltpu.VMEM((rows * PACK, LANES), BF16)],
        (far_ints, far_flat),
        1,
        "far",
        10**13,
    )
    far, near, from_left, from_right, a_tiles = lax.optimization_barrier(
        (far, near, from_left, from_right, a_tiles)
    )
    far = exchange(far)
    coupling = call(
        coupling_kernel,
        shape(rows, B, pl.cdiv(span, 2) * LANES),
        [pltpu.VMEM((2, rows, PACK, 2 * LANES), f32)],
        (a_tiles.transpose(1, 0, 2),),
        0,
        "coupling",
        2 * 10**9,
    )
    restrict = call(
        functools.partial(restrict_kernel, rows, col_size),
        shape(col_size * CP * B, rows * B),
        [],
        panels,
        0,
        "restrict",
        2 * 10**8,
    )
    partial = call(
        functools.partial(product_kernel, n),
        shape(col_size * CP * B, CP * B, dtype=f32),
        [pltpu.VMEM(((rows + n * S) * B, LANES), BF16), pltpu.VMEM((rows * B, CP * B), BF16)],
        (neighbors.T, near, far, from_left, from_right, own, coupling, restrict),
        1,
        "product",
        2 * 10**8,
    )
    share = col_size * CP * B // n
    parts = lax.all_to_all(
        partial.reshape(n, share, CP * B), "row", split_axis=0, concat_axis=0, tiled=True
    )
    return jnp.sum(parts, axis=0)


def solution(mesh):
    in_specs = (
        P("row", None, None),
        P("row", None),
        P("row", None),
        P("row", "col", None),
        P("row", "col"),
    )
    out_specs = P("row", "col")
    body = functools.partial(shards, mesh.shape["row"], mesh.shape["col"])
    return jax.shard_map(body, mesh=mesh, in_specs=in_specs, out_specs=out_specs, check_vma=False)
```

```python
import functools

import jax
import jax.numpy as jnp
from jax import lax
from jax.experimental import pallas as pl
from jax.experimental.pallas import tpu as pltpu
from jax.sharding import PartitionSpec as P

B = 64
CP = 2
S = 8
S2 = 4
LANES = 128
PACK = B * B // LANES
BF16 = jnp.bfloat16
VMEM = pl.BlockSpec(memory_space=pltpu.VMEM)
SMEM = pl.BlockSpec(memory_space=pltpu.SMEM)
PARAMS = pltpu.CompilerParams(vmem_limit_bytes=40 * 2**20)


def unpack_rows(flat, scratch):
    for l in range(PACK):
        scratch[:, l, :] = flat[:, l * LANES : (l + 1) * LANES].astype(jnp.float32)


def swap_halves(x):
    return jnp.concatenate([x[:, B:], x[:, :B]], axis=1)


def turn_rows(flat, index_of, scratch, out, base):
    rows = scratch.shape[0]
    unpack_rows(flat, scratch)
    for r in range(rows):
        x = scratch[r]
        x = jnp.where(index_of(r) == 0, x, swap_halves(x))
        out[base + r * PACK : base + (r + 1) * PACK, :] = x.astype(BF16)


def mask_row(index, shape):
    lane = lax.broadcasted_iota(jnp.int32, shape, len(shape) - 1)
    return jnp.where((lane >= B) == (index != 0), 1.0, 0.0)


def widen(x, mask):
    return x * mask, swap_halves(x) * mask


def mask_table(index_of, rows):
    sub = lax.broadcasted_iota(jnp.int32, (rows, LANES), 0)
    table = jnp.zeros((rows, LANES), jnp.float32)
    for r in range(rows):
        table = jnp.where(sub == r, mask_row(index_of(r), (rows, LANES)), table)
    return table


def fill(ref, table, picks):
    marks = ref.shape[0] - len(picks) * PACK
    sub = lax.broadcasted_iota(jnp.int32, (marks, LANES), 0)
    mark = jnp.zeros((marks, LANES), jnp.float32)
    for s, (row, index) in enumerate(picks):
        ref[s * PACK : (s + 1) * PACK, :] = table[pl.ds(pl.multiple_of(row * PACK, PACK), PACK), :]
        mark = jnp.where(sub == s, mask_row(index, (marks, LANES)), mark)
    ref[len(picks) * PACK :, :] = mark.astype(BF16)


def beyond(n, me):
    half = n // 2
    low = lax.rem(me, half)
    return me + jnp.where((low == 0) | (low == half - 1), 0, 2 * lax.rem(me, 2) - 1)


def own_kernel(n, send_ref, index_ref, flat_ref, own_ref, pair_ref, edge_ref, restrict_ref, scratch):
    rows = flat_ref.shape[0]
    me = lax.axis_index("row")
    turn_rows(flat_ref, lambda r: index_ref[0, r], scratch, own_ref, 0)
    masks = mask_table(lambda r: index_ref[0, r], rows)
    own_ref[rows * PACK :, :] = masks.astype(BF16)

    def look(slot):
        row = send_ref[0, slot]
        return row, index_ref[0, row]

    fill(edge_ref, own_ref, [look(beyond(n, me) * S + s) for s in range(S2, S)])
    fill(pair_ref, own_ref, [look(lax.bitwise_xor(me, 1) * S + s) for s in range(S)])
    pieces = []
    for r in range(rows):
        x = own_ref[r * PACK : (r + 1) * PACK, :].astype(jnp.float32)
        pieces.extend(widen(x, masks[r : r + 1, :]))
    restrict_ref[...] = jnp.concatenate(pieces, axis=0).T.astype(BF16)


def coupling_kernel(a_ref, coupling_ref, scratch):
    span, rows, _ = a_ref.shape
    src = lax.broadcasted_iota(jnp.int32, (2 * LANES, 2 * LANES), 0)
    dst = lax.broadcasted_iota(jnp.int32, (2 * LANES, 2 * LANES), 1)
    odd, block, part = dst // LANES, lax.rem(dst // B, 2), lax.rem(dst, B)
    column = jnp.where(part < B // 2, 2 * part, 2 * part - B + 1)
    order = (src == block * LANES + odd * B + column).astype(BF16)
    for pair in range(pl.cdiv(span, 2)):
        blocks = range(2 * pair, min(2 * pair + 2, span))
        buffer = scratch.at[pair % 2]
        for k in blocks:
            unpack_rows(a_ref.at[k], buffer.at[:, :, pl.ds((k % 2) * LANES, LANES)])
        width = len(blocks) * LANES
        packed = buffer[:, :, :width].reshape(rows * PACK, width).astype(BF16)
        ordered = jnp.dot(packed, order[:width], preferred_element_type=jnp.float32).astype(BF16)
        lanes = pl.ds(pair * LANES, LANES)
        coupling_ref[:, :PACK, lanes] = ordered[:, :LANES].reshape(rows, PACK, LANES)
        coupling_ref[:, PACK:, lanes] = ordered[:, LANES:].reshape(rows, PACK, LANES)


def pack_kernel(n, steps, send_ref, index_ref, far_ref, own_ref, flat_ref, self_ref, *refs):
    rows = flat_ref.shape[0]
    out_refs, (scratch, table) = refs[: len(steps)], refs[len(steps) :]
    me = lax.axis_index("row")
    turn_rows(flat_ref, lambda r: far_ref[0, n * S + r], scratch, table, rows * PACK)
    table[: rows * PACK, :] = own_ref[: rows * PACK, :]

    def near_row(slot):
        row = send_ref[0, slot]
        return row, index_ref[0, row]

    def far_row(slot):
        row = far_ref[0, slot]
        return rows + row, far_ref[0, n * S + row]

    for step, ref in zip(steps, out_refs):
        first = lax.bitwise_xor(me, step) * S
        picks = [far_row(first + s) for s in range(S2)]
        if step > 1:
            picks += [near_row(first + s) for s in range(S2)]
        if step == n // 2 - 1:
            picks += [far_row(first + s) for s in range(S2, S)]
        fill(ref, table, picks)
    fill(self_ref, table, [far_row(me * S + s) for s in range(S2)])


def product_kernel(n, col_size, steps, code_ref, self_ref, pair_ref, edge_ref, *refs):
    message_refs, refs = refs[: len(steps)], refs[len(steps) :]
    own_ref, coupling_ref, *restrict_refs, out_ref, wide, ap = refs
    rows = coupling_ref.shape[0]
    span = code_ref.shape[0]
    me = lax.axis_index("row")

    def place(slot, tile, mask):
        even, odd = widen(tile, mask)
        to = pl.multiple_of(slot * B, B)
        wide[pl.ds(to, PACK), :] = even
        wide[pl.ds(pl.multiple_of(to + PACK, PACK), PACK), :] = odd

    def place_slots(ref, firsts):
        for i, first in enumerate(firsts):
            for s in range(S2):
                slot = i * S2 + s
                mask_at = len(firsts) * S2 * PACK + slot
                place(rows + first + s, ref[slot * PACK : (slot + 1) * PACK, :], ref[mask_at : mask_at + 1, :])

    for r in range(rows):
        place(r, own_ref[r * PACK : (r + 1) * PACK, :], own_ref[rows * PACK + r : rows * PACK + r + 1, :])
    place_slots(self_ref, [lax.bitwise_xor(me, n // 2) * S])
    near = lax.bitwise_xor(me, 1) * S
    place_slots(pair_ref, [near, near + S2])
    place_slots(edge_ref, [beyond(n, me) * S + S2])
    for ref, step in zip(message_refs, steps):
        near = lax.bitwise_xor(me, step)
        firsts = [lax.bitwise_xor(near, n // 2) * S]
        if step > 1:
            firsts.append(near * S)
        if step == n // 2 - 1:
            firsts.append(firsts[0] + S2)
        place_slots(ref, firsts)

    def row_body(r, carry):
        picked = jnp.concatenate(
            [wide[pl.ds(pl.multiple_of(code_ref[k, r] * B, B), B), :] for k in range(span)], axis=0
        )
        block = jnp.dot(coupling_ref[r, :, : span * B], picked, preferred_element_type=jnp.float32)
        ap[pl.ds(pl.multiple_of(r * B, B), B), :] = block.astype(BF16)
        return carry

    lax.fori_loop(0, rows, row_body, 0, unroll=8)
    mine = lax.axis_index("col")
    for j, restrict_ref in enumerate(restrict_refs):
        first = lax.rem(mine + col_size - j, col_size) * CP * B
        out_ref[pl.ds(pl.multiple_of(first, LANES), CP * B), :] = jnp.dot(
            restrict_ref[...], ap[...], preferred_element_type=jnp.float32
        )


def shards(n, col_size, a_tiles, neighbors, send_rows, p_tiles, p_index):
    rows, span = a_tiles.shape[0], a_tiles.shape[1]
    half = n // 2
    f32 = jnp.float32
    flat = p_tiles[:, 0, :]
    index = p_index.T

    def call(body, out_shape, scratch_shapes, operands, smem, name, flops=10**7):
        return pl.pallas_call(
            body,
            out_shape=out_shape,
            in_specs=[SMEM] * smem + [VMEM] * (len(operands) - smem),
            out_specs=jax.tree.map(lambda _: VMEM, out_shape),
            scratch_shapes=scratch_shapes,
            compiler_params=PARAMS,
            cost_estimate=pl.CostEstimate(flops=flops, bytes_accessed=2**20, transcendentals=0),
            name=name,
        )(*operands)

    def shape(*dims, dtype=BF16):
        return jax.ShapeDtypeStruct(dims, dtype)

    def message(slots):
        return shape(slots * PACK + (8 if slots <= 8 else 16), LANES)

    def swap(x, bits):
        return lax.ppermute(x, "row", [(i, i ^ bits) for i in range(n)])

    unpacked = pltpu.VMEM((rows, PACK, LANES), f32)
    far_flat = swap(flat, half)
    far_ints = swap(jnp.concatenate([send_rows, index], axis=1), half)
    own, pair, edge, restrict = call(
        functools.partial(own_kernel, n),
        [shape(rows * PACK + rows, LANES), message(S), message(S2), shape(CP * B, rows * B)],
        [unpacked],
        (send_rows, index, flat),
        2,
        "own",
    )
    pair = swap(pair, 1)
    edge = lax.ppermute(edge, "row", [(i, i + 2 * (i % 2) - 1) for i in range(n) if 0 < i % half < half - 1])
    restricts = [restrict] + [
        lax.ppermute(restrict, "col", [(i, (i + j) % col_size) for i in range(col_size)])
        for j in range(1, col_size)
    ]
    coupling = call(
        coupling_kernel,
        shape(rows, B, pl.cdiv(span, 2) * LANES),
        [pltpu.VMEM((2, rows, PACK, 2 * LANES), f32)],
        (a_tiles.transpose(1, 0, 2),),
        0,
        "coupling",
    )
    far_flat, far_ints, pair, edge, coupling = lax.optimization_barrier(
        (far_flat, far_ints, pair, edge, coupling)
    )
    steps = sorted(range(1, half), key=lambda d: (d == 1, -d.bit_count(), 1 - d % 2, -d))
    self_part, *out = call(
        functools.partial(pack_kernel, n, steps),
        [message(S2)] + [message((3 if step == half - 1 else 1 + (step > 1)) * S2) for step in steps],
        [unpacked, pltpu.VMEM((2 * rows * PACK, LANES), BF16)],
        (send_rows, index, far_ints, own, far_flat),
        3,
        "pack",
    )
    messages = [swap(x, step) for x, step in zip(out, steps)]
    partial = call(
        functools.partial(product_kernel, n, col_size, steps),
        shape(col_size * CP * B, CP * B, dtype=f32),
        [pltpu.VMEM(((rows + n * S) * B, LANES), BF16), pltpu.VMEM((rows * B, CP * B), BF16)],
        (neighbors.T, self_part, pair, edge, *messages, own, coupling, *restricts),
        1,
        "product",
        2 * 10**8,
    )
    share = col_size * CP * B // n
    parts = lax.all_to_all(
        partial.reshape(n, share, CP * B), "row", split_axis=0, concat_axis=0, tiled=True
    )
    return jnp.sum(parts, axis=0)


def solution(mesh):
    in_specs = (
        P("row", None, None),
        P("row", None),
        P("row", None),
        P("row", "col", None),
        P("row", "col"),
    )
    out_specs = P("row", "col")
    body = functools.partial(shards, mesh.shape["row"], mesh.shape["col"])
    return jax.shard_map(body, mesh=mesh, in_specs=in_specs, out_specs=out_specs, check_vma=False)
```

```python
import functools

import jax
import jax.numpy as jnp
from jax import lax
from jax.experimental import pallas as pl
from jax.experimental.pallas import tpu as pltpu
from jax.sharding import PartitionSpec as P

B = 64
CP = 2
S = 8
S2 = 4
LANES = 128
PACK = B * B // LANES
BF16 = jnp.bfloat16
VMEM = pl.BlockSpec(memory_space=pltpu.VMEM)
SMEM = pl.BlockSpec(memory_space=pltpu.SMEM)
PARAMS = pltpu.CompilerParams(vmem_limit_bytes=40 * 2**20)


def unpack_rows(flat, scratch):
    for l in range(PACK):
        scratch[:, l, :] = flat[:, l * LANES : (l + 1) * LANES].astype(jnp.float32)


def swap_halves(x):
    return jnp.concatenate([x[:, B:], x[:, :B]], axis=1)


def turn_rows(flat, index_of, scratch, out, base):
    rows = scratch.shape[0]
    unpack_rows(flat, scratch)
    for r in range(rows):
        x = scratch[r]
        x = jnp.where(index_of(r) == 0, x, swap_halves(x))
        out[base + r * PACK : base + (r + 1) * PACK, :] = x.astype(BF16)


def mask_row(index, shape):
    lane = lax.broadcasted_iota(jnp.int32, shape, len(shape) - 1)
    return jnp.where((lane >= B) == (index != 0), 1.0, 0.0)


def widen(x, mask):
    return x * mask, swap_halves(x) * mask


def mask_table(index_of, rows):
    sub = lax.broadcasted_iota(jnp.int32, (rows, LANES), 0)
    table = jnp.zeros((rows, LANES), jnp.float32)
    for r in range(rows):
        table = jnp.where(sub == r, mask_row(index_of(r), (rows, LANES)), table)
    return table


def fill(ref, table, picks):
    marks = ref.shape[0] - len(picks) * PACK
    sub = lax.broadcasted_iota(jnp.int32, (marks, LANES), 0)
    mark = jnp.zeros((marks, LANES), jnp.float32)
    for s, (row, index) in enumerate(picks):
        ref[s * PACK : (s + 1) * PACK, :] = table[pl.ds(pl.multiple_of(row * PACK, PACK), PACK), :]
        mark = jnp.where(sub == s, mask_row(index, (marks, LANES)), mark)
    ref[len(picks) * PACK :, :] = mark.astype(BF16)


def prepare_kernel(col_size, *refs):
    index_refs, refs = refs[:col_size], refs[col_size:]
    flat_refs, refs = refs[:col_size], refs[col_size:]
    own_ref, restrict_ref, scratch, table = refs
    rows = flat_refs[0].shape[0]
    mine = lax.axis_index("col")
    for j, (index_ref, flat_ref) in enumerate(zip(index_refs, flat_refs)):
        panel = lax.rem(mine + col_size - j, col_size)
        turned = own_ref if j == 0 else table

        def index_of(r, index_ref=index_ref):
            return index_ref[0, r]

        turn_rows(flat_ref, index_of, scratch, turned, 0)
        masks = mask_table(index_of, rows)
        if j == 0:
            own_ref[rows * PACK :, :] = masks.astype(BF16)
        pieces = []
        for r in range(rows):
            x = turned[r * PACK : (r + 1) * PACK, :].astype(jnp.float32)
            pieces.extend(widen(x, masks[r : r + 1, :]))
        wide = jnp.concatenate(pieces, axis=0)
        restrict_ref[pl.ds(pl.multiple_of(panel * CP * B, LANES), CP * B), :] = wide.T.astype(BF16)


def coupling_kernel(a_ref, coupling_ref, scratch):
    span, rows, _ = a_ref.shape
    src = lax.broadcasted_iota(jnp.int32, (2 * LANES, 2 * LANES), 0)
    dst = lax.broadcasted_iota(jnp.int32, (2 * LANES, 2 * LANES), 1)
    odd, block, part = dst // LANES, lax.rem(dst // B, 2), lax.rem(dst, B)
    column = jnp.where(part < B // 2, 2 * part, 2 * part - B + 1)
    order = (src == block * LANES + odd * B + column).astype(BF16)
    for pair in range(pl.cdiv(span, 2)):
        blocks = range(2 * pair, min(2 * pair + 2, span))
        buffer = scratch.at[pair % 2]
        for k in blocks:
            unpack_rows(a_ref.at[k], buffer.at[:, :, pl.ds((k % 2) * LANES, LANES)])
        width = len(blocks) * LANES
        packed = buffer[:, :, :width].reshape(rows * PACK, width).astype(BF16)
        ordered = jnp.dot(packed, order[:width], preferred_element_type=jnp.float32).astype(BF16)
        lanes = pl.ds(pair * LANES, LANES)
        coupling_ref[:, :PACK, lanes] = ordered[:, :LANES].reshape(rows, PACK, LANES)
        coupling_ref[:, PACK:, lanes] = ordered[:, LANES:].reshape(rows, PACK, LANES)


def beside(n, p, q):
    gap = lax.rem(p - q + n, n)
    return (gap == 1) | (gap == n - 1)


def has_edge(step):
    return step & (step + 1) == 0


def message_order(half):
    edges = sorted((d for d in range(1, half) if has_edge(d)), reverse=True)
    rest = sorted((d for d in range(1, half) if not has_edge(d)), key=lambda d: (-d.bit_count(), -(d % 2), d))
    return rest[: len(rest) // 2] + edges + rest[len(rest) // 2 :]


def pack_kernel(n, steps, send_ref, index_ref, far_ref, own_ref, flat_ref, self_ref, *refs):
    rows = flat_ref.shape[0]
    out_refs, (scratch, table) = refs[: len(steps)], refs[len(steps) :]
    me = lax.axis_index("row")
    turn_rows(flat_ref, lambda r: far_ref[0, n * S + r], scratch, table, rows * PACK)
    table[: rows * PACK, :] = own_ref[: rows * PACK, :]

    def near_row(slot):
        row = send_ref[0, slot]
        return row, index_ref[0, row]

    def far_row(slot):
        row = far_ref[0, slot]
        return rows + row, far_ref[0, n * S + row]

    for step, ref in zip(steps, out_refs):
        target = lax.bitwise_xor(me, step)
        first = target * S
        picks = [near_row(first + s) for s in range(S2)] + [far_row(first + s) for s in range(S2)]
        if has_edge(step):
            near = beside(n, me, target)
            for s in range(S2, S):
                pairs = zip(near_row(first + s), far_row(first + s))
                picks.append(tuple(jnp.where(near, x, y) for x, y in pairs))
        fill(ref, table, picks)
    fill(self_ref, table, [far_row(me * S + s) for s in range(S2)])


def product_kernel(n, steps, code_ref, self_ref, *refs):
    message_refs, refs = refs[: len(steps)], refs[len(steps) :]
    own_ref, coupling_ref, restrict_ref, out_ref, wide, ap = refs
    rows = coupling_ref.shape[0]
    span = code_ref.shape[0]
    me = lax.axis_index("row")

    def place(slot, tile, mask):
        even, odd = widen(tile, mask)
        to = pl.multiple_of(slot * B, B)
        wide[pl.ds(to, PACK), :] = even
        wide[pl.ds(pl.multiple_of(to + PACK, PACK), PACK), :] = odd

    def place_slots(ref, firsts):
        for i, first in enumerate(firsts):
            for s in range(S2):
                slot = i * S2 + s
                mask_at = len(firsts) * S2 * PACK + slot
                place(rows + first + s, ref[slot * PACK : (slot + 1) * PACK, :], ref[mask_at : mask_at + 1, :])

    for r in range(rows):
        place(r, own_ref[r * PACK : (r + 1) * PACK, :], own_ref[rows * PACK + r : rows * PACK + r + 1, :])
    place_slots(self_ref, [lax.bitwise_xor(me, n // 2) * S])
    for ref, step in zip(message_refs, steps):
        near = lax.bitwise_xor(me, step)
        far = lax.bitwise_xor(near, n // 2)
        firsts = [near * S, far * S]
        if has_edge(step):
            firsts.append(jnp.where(beside(n, me, near), near, far) * S + S2)
        place_slots(ref, firsts)

    def row_body(r, carry):
        picked = jnp.concatenate(
            [wide[pl.ds(pl.multiple_of(code_ref[k, r] * B, B), B), :] for k in range(span)], axis=0
        )
        block = jnp.dot(coupling_ref[r, :, : span * B], picked, preferred_element_type=jnp.float32)
        ap[pl.ds(pl.multiple_of(r * B, B), B), :] = block.astype(BF16)
        return carry

    lax.fori_loop(0, rows, row_body, 0, unroll=8)
    out_ref[...] = jnp.dot(restrict_ref[...], ap[...], preferred_element_type=jnp.float32).astype(BF16)


def shards(n, col_size, a_tiles, neighbors, send_rows, p_tiles, p_index):
    rows, span = a_tiles.shape[0], a_tiles.shape[1]
    half = n // 2
    f32 = jnp.float32
    flat = p_tiles[:, 0, :]
    index = p_index.T

    def call(body, out_shape, scratch_shapes, operands, smem, name, flops=10**7):
        return pl.pallas_call(
            body,
            out_shape=out_shape,
            in_specs=[SMEM] * smem + [VMEM] * (len(operands) - smem),
            out_specs=jax.tree.map(lambda _: VMEM, out_shape),
            scratch_shapes=scratch_shapes,
            compiler_params=PARAMS,
            cost_estimate=pl.CostEstimate(flops=flops, bytes_accessed=2**20, transcendentals=0),
            name=name,
        )(*operands)

    def shape(*dims, dtype=BF16):
        return jax.ShapeDtypeStruct(dims, dtype)

    def message(slots):
        return shape(slots * PACK + (8 if slots <= 8 else 16), LANES)

    def swap(x, bits):
        return lax.ppermute(x, "row", [(i, i ^ bits) for i in range(n)])

    unpacked = pltpu.VMEM((rows, PACK, LANES), f32)
    far_flat = swap(flat, half)
    far_ints = swap(jnp.concatenate([send_rows, index], axis=1), half)
    flats, indices = [flat], [index]
    for j in range(1, col_size):
        turn = [(i, (i + j) % col_size) for i in range(col_size)]
        flats.append(lax.ppermute(flat, "col", turn))
        indices.append(lax.ppermute(index, "col", turn))
    own, restrict = call(
        functools.partial(prepare_kernel, col_size),
        [shape(rows * PACK + rows, LANES), shape(col_size * CP * B, rows * B)],
        [unpacked, pltpu.VMEM((rows * PACK, LANES), BF16)],
        (*indices, *flats),
        col_size,
        "prepare",
    )
    coupling = call(
        coupling_kernel,
        shape(rows, B, pl.cdiv(span, 2) * LANES),
        [pltpu.VMEM((2, rows, PACK, 2 * LANES), f32)],
        (a_tiles.transpose(1, 0, 2),),
        0,
        "coupling",
    )
    far_flat, far_ints, coupling, own = lax.optimization_barrier((far_flat, far_ints, coupling, own))
    steps = message_order(half)
    self_part, *out = call(
        functools.partial(pack_kernel, n, steps),
        [message(S2)] + [message((3 if has_edge(step) else 2) * S2) for step in steps],
        [unpacked, pltpu.VMEM((2 * rows * PACK, LANES), BF16)],
        (send_rows, index, far_ints, own, far_flat),
        3,
        "pack",
    )
    messages = [swap(x, step) for x, step in zip(out, steps)]
    partial = call(
        functools.partial(product_kernel, n, steps),
        shape(col_size * CP * B, CP * B),
        [pltpu.VMEM(((rows + n * S) * B, LANES), BF16), pltpu.VMEM((rows * B, CP * B), BF16)],
        (neighbors.T, self_part, *messages, own, coupling, restrict),
        1,
        "product",
        2 * 10**8,
    )
    share = col_size * CP * B // n
    parts = lax.all_to_all(
        partial.reshape(n, share, CP * B), "row", split_axis=0, concat_axis=0, tiled=True
    )
    return jnp.sum(parts.astype(f32), axis=0)


def solution(mesh):
    in_specs = (
        P("row", None, None),
        P("row", None),
        P("row", None),
        P("row", "col", None),
        P("row", "col"),
    )
    out_specs = P("row", "col")
    body = functools.partial(shards, mesh.shape["row"], mesh.shape["col"])
    return jax.shard_map(body, mesh=mesh, in_specs=in_specs, out_specs=out_specs, check_vma=False)
```

```python
import functools

import jax
import jax.numpy as jnp
from jax import lax
from jax.experimental import pallas as pl
from jax.experimental.pallas import tpu as pltpu
from jax.sharding import PartitionSpec as P

B = 64
CP = 2
S = 8
S2 = 4
LANES = 128
PACK = B * B // LANES
BF16 = jnp.bfloat16
VMEM = pl.BlockSpec(memory_space=pltpu.VMEM)
SMEM = pl.BlockSpec(memory_space=pltpu.SMEM)
PARAMS = pltpu.CompilerParams(vmem_limit_bytes=40 * 2**20)


def unpack_rows(flat, scratch):
    for l in range(PACK):
        scratch[:, l, :] = flat[:, l * LANES : (l + 1) * LANES].astype(jnp.float32)


def swap_halves(x):
    return jnp.concatenate([x[:, B:], x[:, :B]], axis=1)


def turn_rows(flat, index_of, scratch, out, base):
    rows = scratch.shape[0]
    unpack_rows(flat, scratch)
    for r in range(rows):
        x = scratch[r]
        x = jnp.where(index_of(r) == 0, x, swap_halves(x))
        out[base + r * PACK : base + (r + 1) * PACK, :] = x.astype(BF16)


def mask_row(index, shape):
    lane = lax.broadcasted_iota(jnp.int32, shape, len(shape) - 1)
    return jnp.where((lane >= B) == (index != 0), 1.0, 0.0)


def widen(x, mask):
    return x * mask, swap_halves(x) * mask


def mask_table(index_of, rows):
    sub = lax.broadcasted_iota(jnp.int32, (rows, LANES), 0)
    table = jnp.zeros((rows, LANES), jnp.float32)
    for r in range(rows):
        table = jnp.where(sub == r, mask_row(index_of(r), (rows, LANES)), table)
    return table


def fill(ref, table, picks):
    marks = ref.shape[0] - len(picks) * PACK
    sub = lax.broadcasted_iota(jnp.int32, (marks, LANES), 0)
    mark = jnp.zeros((marks, LANES), jnp.float32)
    for s, (row, index) in enumerate(picks):
        ref[s * PACK : (s + 1) * PACK, :] = table[pl.ds(pl.multiple_of(row * PACK, PACK), PACK), :]
        mark = jnp.where(sub == s, mask_row(index, (marks, LANES)), mark)
    ref[len(picks) * PACK :, :] = mark.astype(BF16)


def prepare_kernel(n, col_size, send_ref, *refs):
    index_refs, refs = refs[:col_size], refs[col_size:]
    flat_refs, refs = refs[:col_size], refs[col_size:]
    own_ref, pair_ref, restrict_ref, scratch, table = refs
    rows = flat_refs[0].shape[0]
    pair = lax.bitwise_xor(lax.axis_index("row"), 1) * S
    mine = lax.axis_index("col")
    for j, (index_ref, flat_ref) in enumerate(zip(index_refs, flat_refs)):
        panel = lax.rem(mine + col_size - j, col_size)
        turned = own_ref if j == 0 else table

        def index_of(r, index_ref=index_ref):
            return index_ref[0, r]

        turn_rows(flat_ref, index_of, scratch, turned, 0)
        masks = mask_table(index_of, rows)
        if j == 0:
            own_ref[rows * PACK :, :] = masks.astype(BF16)
            slots = [send_ref[0, pair + s] for s in range(S)]
            fill(pair_ref, own_ref, [(row, index_of(row)) for row in slots])
        pieces = []
        for r in range(rows):
            x = turned[r * PACK : (r + 1) * PACK, :].astype(jnp.float32)
            pieces.extend(widen(x, masks[r : r + 1, :]))
        wide = jnp.concatenate(pieces, axis=0)
        restrict_ref[pl.ds(pl.multiple_of(panel * CP * B, LANES), CP * B), :] = wide.T.astype(BF16)


def coupling_kernel(a_ref, coupling_ref, scratch):
    span, rows, _ = a_ref.shape
    src = lax.broadcasted_iota(jnp.int32, (2 * LANES, 2 * LANES), 0)
    dst = lax.broadcasted_iota(jnp.int32, (2 * LANES, 2 * LANES), 1)
    odd, block, part = dst // LANES, lax.rem(dst // B, 2), lax.rem(dst, B)
    column = jnp.where(part < B // 2, 2 * part, 2 * part - B + 1)
    order = (src == block * LANES + odd * B + column).astype(BF16)
    for pair in range(pl.cdiv(span, 2)):
        blocks = range(2 * pair, min(2 * pair + 2, span))
        buffer = scratch.at[pair % 2]
        for k in blocks:
            unpack_rows(a_ref.at[k], buffer.at[:, :, pl.ds((k % 2) * LANES, LANES)])
        width = len(blocks) * LANES
        packed = buffer[:, :, :width].reshape(rows * PACK, width).astype(BF16)
        ordered = jnp.dot(packed, order[:width], preferred_element_type=jnp.float32).astype(BF16)
        lanes = pl.ds(pair * LANES, LANES)
        coupling_ref[:, :PACK, lanes] = ordered[:, :LANES].reshape(rows, PACK, LANES)
        coupling_ref[:, PACK:, lanes] = ordered[:, LANES:].reshape(rows, PACK, LANES)


def other_neighbour(half, me):
    low = lax.rem(me, half)
    odd = lax.rem(me, 2) == 1
    return me - low + lax.rem(low + jnp.where(odd, 1, half - 1), half)


def at_end(half, me):
    low = lax.rem(me, half)
    return (low == 0) | (low == half - 1)


def pack_kernel(n, steps, send_ref, index_ref, far_ref, own_ref, flat_ref, self_ref, edge_ref, *refs):
    rows = flat_ref.shape[0]
    out_refs, (scratch, table) = refs[: len(steps)], refs[len(steps) :]
    me = lax.axis_index("row")
    turn_rows(flat_ref, lambda r: far_ref[0, n * S + r], scratch, table, rows * PACK)
    table[: rows * PACK, :] = own_ref[: rows * PACK, :]

    def near_row(slot):
        row = send_ref[0, slot]
        return row, index_ref[0, row]

    def far_row(slot):
        row = far_ref[0, slot]
        return rows + row, far_ref[0, n * S + row]

    for step, ref in zip(steps, out_refs):
        first = lax.bitwise_xor(me, step) * S
        picks = [far_row(first + s) for s in range(S2)]
        if step > 1:
            picks += [near_row(first + s) for s in range(S2)]
        fill(ref, table, picks)
    first = other_neighbour(n // 2, me) * S
    picks = []
    for s in range(S2, S):
        pairs = zip(far_row(first + s), near_row(first + s))
        picks.append(tuple(jnp.where(at_end(n // 2, me), x, y) for x, y in pairs))
    fill(edge_ref, table, picks)
    fill(self_ref, table, [far_row(me * S + s) for s in range(S2)])


def product_kernel(n, steps, code_ref, self_ref, edge_ref, pair_ref, *refs):
    message_refs, refs = refs[: len(steps)], refs[len(steps) :]
    own_ref, coupling_ref, restrict_ref, out_ref, wide, ap = refs
    rows = coupling_ref.shape[0]
    span = code_ref.shape[0]
    me = lax.axis_index("row")

    def place(slot, tile, mask):
        even, odd = widen(tile, mask)
        to = pl.multiple_of(slot * B, B)
        wide[pl.ds(to, PACK), :] = even
        wide[pl.ds(pl.multiple_of(to + PACK, PACK), PACK), :] = odd

    def place_slots(ref, firsts):
        for i, first in enumerate(firsts):
            for s in range(S2):
                slot = i * S2 + s
                mask_at = len(firsts) * S2 * PACK + slot
                place(rows + first + s, ref[slot * PACK : (slot + 1) * PACK, :], ref[mask_at : mask_at + 1, :])

    for r in range(rows):
        place(r, own_ref[r * PACK : (r + 1) * PACK, :], own_ref[rows * PACK + r : rows * PACK + r + 1, :])
    place_slots(self_ref, [lax.bitwise_xor(me, n // 2) * S])
    near = lax.bitwise_xor(me, 1) * S
    place_slots(pair_ref, [near, near + S2])
    near = other_neighbour(n // 2, me)
    place_slots(edge_ref, [jnp.where(at_end(n // 2, me), lax.bitwise_xor(near, n // 2), near) * S + S2])
    for ref, step in zip(message_refs, steps):
        near = lax.bitwise_xor(me, step)
        firsts = [lax.bitwise_xor(near, n // 2) * S]
        if step > 1:
            firsts.append(near * S)
        place_slots(ref, firsts)

    def row_body(r, carry):
        picked = jnp.concatenate(
            [wide[pl.ds(pl.multiple_of(code_ref[k, r] * B, B), B), :] for k in range(span)], axis=0
        )
        block = jnp.dot(coupling_ref[r, :, : span * B], picked, preferred_element_type=jnp.float32)
        ap[pl.ds(pl.multiple_of(r * B, B), B), :] = block.astype(BF16)
        return carry

    lax.fori_loop(0, rows, row_body, 0, unroll=8)
    out_ref[...] = jnp.dot(restrict_ref[...], ap[...], preferred_element_type=jnp.float32)


def shards(n, col_size, a_tiles, neighbors, send_rows, p_tiles, p_index):
    rows, span = a_tiles.shape[0], a_tiles.shape[1]
    half = n // 2
    f32 = jnp.float32
    flat = p_tiles[:, 0, :]
    index = p_index.T

    def call(body, out_shape, scratch_shapes, operands, smem, name, flops=10**7):
        return pl.pallas_call(
            body,
            out_shape=out_shape,
            in_specs=[SMEM] * smem + [VMEM] * (len(operands) - smem),
            out_specs=jax.tree.map(lambda _: VMEM, out_shape),
            scratch_shapes=scratch_shapes,
            compiler_params=PARAMS,
            cost_estimate=pl.CostEstimate(flops=flops, bytes_accessed=2**20, transcendentals=0),
            name=name,
        )(*operands)

    def shape(*dims, dtype=BF16):
        return jax.ShapeDtypeStruct(dims, dtype)

    def message(slots):
        return shape(slots * PACK + 8, LANES)

    def swap(x, bits):
        return lax.ppermute(x, "row", [(i, i ^ bits) for i in range(n)])

    unpacked = pltpu.VMEM((rows, PACK, LANES), f32)
    far_flat = swap(flat, half)
    far_ints = swap(jnp.concatenate([send_rows, index], axis=1), half)
    flats, indices = [flat], [index]
    for j in range(1, col_size):
        turn = [(i, (i + j) % col_size) for i in range(col_size)]
        flats.append(lax.ppermute(flat, "col", turn))
        indices.append(lax.ppermute(index, "col", turn))
    own, pair, restrict = call(
        functools.partial(prepare_kernel, n, col_size),
        [shape(rows * PACK + rows, LANES), message(S), shape(col_size * CP * B, rows * B)],
        [unpacked, pltpu.VMEM((rows * PACK, LANES), BF16)],
        (send_rows, *indices, *flats),
        1 + col_size,
        "prepare",
    )
    coupling = call(
        coupling_kernel,
        shape(rows, B, pl.cdiv(span, 2) * LANES),
        [pltpu.VMEM((2, rows, PACK, 2 * LANES), f32)],
        (a_tiles.transpose(1, 0, 2),),
        0,
        "coupling",
    )
    far_flat, far_ints, coupling, own = lax.optimization_barrier((far_flat, far_ints, coupling, own))
    steps = sorted(range(1, half), key=lambda d: (d == 1, -d.bit_count(), 1 - d % 2, -d))
    self_part, edge, *out = call(
        functools.partial(pack_kernel, n, steps),
        [message(S2)] * 2 + [message((2 if step > 1 else 1) * S2) for step in steps],
        [unpacked, pltpu.VMEM((2 * rows * PACK, LANES), BF16)],
        (send_rows, index, far_ints, own, far_flat),
        3,
        "pack",
    )
    pair, edge, *out = lax.optimization_barrier((swap(pair, 1), edge, *out))
    messages = [swap(x, step) for x, step in zip(out, steps)]
    ends = [i % 2 * 2 - 1 for i in range(half)]
    edge = lax.ppermute(
        edge, "row", [(g + i, g + (i + ends[i]) % half) for g in (0, half) for i in range(half)]
    )
    partial = call(
        functools.partial(product_kernel, n, steps),
        shape(col_size * CP * B, CP * B, dtype=f32),
        [pltpu.VMEM(((rows + n * S) * B, LANES), BF16), pltpu.VMEM((rows * B, CP * B), BF16)],
        (neighbors.T, self_part, edge, pair, *messages, own, coupling, restrict),
        1,
        "product",
        2 * 10**8,
    )
    share = col_size * CP * B // n
    parts = lax.all_to_all(
        partial.reshape(n, share, CP * B), "row", split_axis=0, concat_axis=0, tiled=True
    )
    return jnp.sum(parts, axis=0)


def solution(mesh):
    in_specs = (
        P("row", None, None),
        P("row", None),
        P("row", None),
        P("row", "col", None),
        P("row", "col"),
    )
    out_specs = P("row", "col")
    body = functools.partial(shards, mesh.shape["row"], mesh.shape["col"])
    return jax.shard_map(body, mesh=mesh, in_specs=in_specs, out_specs=out_specs, check_vma=False)
```

```python
import functools

import jax
import jax.numpy as jnp
from jax import lax
from jax.experimental import pallas as pl
from jax.experimental.pallas import tpu as pltpu
from jax.sharding import PartitionSpec as P

B = 64
CP = 2
S = 8
S2 = 4
LANES = 128
PACK = B * B // LANES
BF16 = jnp.bfloat16
VMEM = pl.BlockSpec(memory_space=pltpu.VMEM)
SMEM = pl.BlockSpec(memory_space=pltpu.SMEM)
HBM = pl.BlockSpec(memory_space=pl.ANY)
PARAMS = pltpu.CompilerParams(vmem_limit_bytes=40 * 2**20)


def unpack_rows(flat, scratch):
    for l in range(PACK):
        scratch[:, l, :] = flat[:, l * LANES : (l + 1) * LANES].astype(jnp.float32)


def swap_halves(x):
    return jnp.concatenate([x[:, B:], x[:, :B]], axis=1)


def turn_rows(index_of, scratch, out, base):
    rows = scratch.shape[0]
    for r in range(rows):
        x = scratch[r]
        x = jnp.where(index_of(r) == 0, x, swap_halves(x))
        out[base + r * PACK : base + (r + 1) * PACK, :] = x.astype(BF16)


def mask_row(index, shape):
    lane = lax.broadcasted_iota(jnp.int32, shape, len(shape) - 1)
    return jnp.where((lane >= B) == (index != 0), 1.0, 0.0)


def widen(x, mask):
    return x * mask, swap_halves(x) * mask


def mask_table(index_of, rows):
    sub = lax.broadcasted_iota(jnp.int32, (rows, LANES), 0)
    table = jnp.zeros((rows, LANES), jnp.float32)
    for r in range(rows):
        table = jnp.where(sub == r, mask_row(index_of(r), (rows, LANES)), table)
    return table


def fill(ref, table, picks):
    marks = ref.shape[0] - len(picks) * PACK
    sub = lax.broadcasted_iota(jnp.int32, (marks, LANES), 0)
    mark = jnp.zeros((marks, LANES), jnp.float32)
    for s, (row, index) in enumerate(picks):
        ref[s * PACK : (s + 1) * PACK, :] = table[pl.ds(pl.multiple_of(row * PACK, PACK), PACK), :]
        mark = jnp.where(sub == s, mask_row(index, (marks, LANES)), mark)
    ref[len(picks) * PACK :, :] = mark.astype(BF16)


def prepare_kernel(col_size, *refs):
    index_refs, refs = refs[:col_size], refs[col_size:]
    flat_refs, refs = refs[:col_size], refs[col_size:]
    own_ref, restrict_ref, scratch, table = refs
    rows = flat_refs[0].shape[0]
    mine = lax.axis_index("col")
    for j, (index_ref, flat_ref) in enumerate(zip(index_refs, flat_refs)):
        panel = lax.rem(mine + col_size - j, col_size)
        turned = own_ref if j == 0 else table

        def index_of(r, index_ref=index_ref):
            return index_ref[0, r]

        unpack_rows(flat_ref, scratch)
        turn_rows(index_of, scratch, turned, 0)
        masks = mask_table(index_of, rows)
        if j == 0:
            own_ref[rows * PACK :, :] = masks.astype(BF16)
        pieces = []
        for r in range(rows):
            x = turned[r * PACK : (r + 1) * PACK, :].astype(jnp.float32)
            pieces.extend(widen(x, masks[r : r + 1, :]))
        wide = jnp.concatenate(pieces, axis=0)
        restrict_ref[pl.ds(pl.multiple_of(panel * CP * B, LANES), CP * B), :] = wide.T.astype(BF16)


def coupling_kernel(a_ref, coupling_ref, scratch):
    span, rows, _ = a_ref.shape
    src = lax.broadcasted_iota(jnp.int32, (2 * LANES, 2 * LANES), 0)
    dst = lax.broadcasted_iota(jnp.int32, (2 * LANES, 2 * LANES), 1)
    odd, block, part = dst // LANES, lax.rem(dst // B, 2), lax.rem(dst, B)
    column = jnp.where(part < B // 2, 2 * part, 2 * part - B + 1)
    order = (src == block * LANES + odd * B + column).astype(BF16)
    for pair in range(pl.cdiv(span, 2)):
        blocks = range(2 * pair, min(2 * pair + 2, span))
        buffer = scratch.at[pair % 2]
        for k in blocks:
            unpack_rows(a_ref.at[k], buffer.at[:, :, pl.ds((k % 2) * LANES, LANES)])
        width = len(blocks) * LANES
        packed = buffer[:, :, :width].reshape(rows * PACK, width).astype(BF16)
        ordered = jnp.dot(packed, order[:width], preferred_element_type=jnp.float32).astype(BF16)
        lanes = pl.ds(pair * LANES, LANES)
        coupling_ref[:, :PACK, lanes] = ordered[:, :LANES].reshape(rows, PACK, LANES)
        coupling_ref[:, PACK:, lanes] = ordered[:, LANES:].reshape(rows, PACK, LANES)


def beside(n, p, q):
    gap = lax.rem(p - q + n, n)
    return (gap == 1) | (gap == n - 1)


def has_edge(step):
    return step & (step + 1) == 0


def message_order(half):
    edges = sorted((d for d in range(1, half) if has_edge(d)), reverse=True)
    rest = sorted((d for d in range(1, half) if not has_edge(d)), key=lambda d: (-d.bit_count(), -(d % 2), d))
    return rest[: len(rest) // 2] + edges + rest[len(rest) // 2 :]


def fetch(sources, targets, sems):
    copies = [pltpu.make_async_copy(x, y, sems.at[i]) for i, (x, y) in enumerate(zip(sources, targets))]
    for copy in copies:
        copy.start()
    return copies


def pack_kernel(n, steps, send_hbm, index_hbm, far_hbm, own_ref, flat_ref, self_ref, *refs):
    rows = flat_ref.shape[0]
    out_refs, (scratch, table, send_ref, index_ref, far_ref, sems) = refs[: len(steps)], refs[len(steps) :]
    copies = fetch((send_hbm, index_hbm, far_hbm), (send_ref, index_ref, far_ref), sems)
    me = lax.axis_index("row")
    unpack_rows(flat_ref, scratch)
    table[: rows * PACK, :] = own_ref[: rows * PACK, :]
    for copy in copies:
        copy.wait()
    turn_rows(lambda r: far_ref[0, n * S + r], scratch, table, rows * PACK)

    def near_row(slot):
        row = send_ref[0, slot]
        return row, index_ref[0, row]

    def far_row(slot):
        row = far_ref[0, slot]
        return rows + row, far_ref[0, n * S + row]

    for step, ref in zip(steps, out_refs):
        target = lax.bitwise_xor(me, step)
        first = target * S
        picks = [near_row(first + s) for s in range(S2)] + [far_row(first + s) for s in range(S2)]
        if has_edge(step):
            near = beside(n, me, target)
            for s in range(S2, S):
                pairs = zip(near_row(first + s), far_row(first + s))
                picks.append(tuple(jnp.where(near, x, y) for x, y in pairs))
        fill(ref, table, picks)
    fill(self_ref, table, [far_row(me * S + s) for s in range(S2)])


def product_kernel(n, steps, code_hbm, self_ref, *refs):
    message_refs, refs = refs[: len(steps)], refs[len(steps) :]
    own_ref, coupling_ref, restrict_ref, out_ref, wide, ap, code_ref, sems = refs
    (copy,) = fetch((code_hbm,), (code_ref,), sems)
    rows = coupling_ref.shape[0]
    span = code_ref.shape[0]
    me = lax.axis_index("row")

    def place(slot, tile, mask):
        even, odd = widen(tile, mask)
        to = pl.multiple_of(slot * B, B)
        wide[pl.ds(to, PACK), :] = even
        wide[pl.ds(pl.multiple_of(to + PACK, PACK), PACK), :] = odd

    def place_slots(ref, firsts):
        for i, first in enumerate(firsts):
            for s in range(S2):
                slot = i * S2 + s
                mask_at = len(firsts) * S2 * PACK + slot
                place(rows + first + s, ref[slot * PACK : (slot + 1) * PACK, :], ref[mask_at : mask_at + 1, :])

    for r in range(rows):
        place(r, own_ref[r * PACK : (r + 1) * PACK, :], own_ref[rows * PACK + r : rows * PACK + r + 1, :])
    place_slots(self_ref, [lax.bitwise_xor(me, n // 2) * S])
    for ref, step in zip(message_refs, steps):
        near = lax.bitwise_xor(me, step)
        far = lax.bitwise_xor(near, n // 2)
        firsts = [near * S, far * S]
        if has_edge(step):
            firsts.append(jnp.where(beside(n, me, near), near, far) * S + S2)
        place_slots(ref, firsts)

    copy.wait()

    def row_body(r, carry):
        picked = jnp.concatenate(
            [wide[pl.ds(pl.multiple_of(code_ref[k, r] * B, B), B), :] for k in range(span)], axis=0
        )
        block = jnp.dot(coupling_ref[r, :, : span * B], picked, preferred_element_type=jnp.float32)
        ap[pl.ds(pl.multiple_of(r * B, B), B), :] = block.astype(BF16)
        return carry

    lax.fori_loop(0, rows, row_body, 0, unroll=8)
    out_ref[...] = jnp.dot(restrict_ref[...], ap[...], preferred_element_type=jnp.float32)


def shards(n, col_size, a_tiles, neighbors, send_rows, p_tiles, p_index):
    rows, span = a_tiles.shape[0], a_tiles.shape[1]
    half = n // 2
    f32 = jnp.float32
    flat = p_tiles[:, 0, :]
    index = p_index.T

    def call(body, out_shape, scratch_shapes, operands, smem, name, hbm=0):
        return pl.pallas_call(
            body,
            out_shape=out_shape,
            in_specs=[SMEM] * smem + [HBM] * hbm + [VMEM] * (len(operands) - smem - hbm),
            out_specs=jax.tree.map(lambda _: VMEM, out_shape),
            scratch_shapes=scratch_shapes,
            compiler_params=PARAMS,
            cost_estimate=pl.CostEstimate(flops=10**7, bytes_accessed=2**20, transcendentals=0),
            name=name,
        )(*operands)

    def shape(*dims, dtype=BF16):
        return jax.ShapeDtypeStruct(dims, dtype)

    def message(slots):
        return shape(slots * PACK + (8 if slots <= 8 else 16), LANES)

    def swap(x, bits):
        return lax.ppermute(x, "row", [(i, i ^ bits) for i in range(n)])

    unpacked = pltpu.VMEM((rows, PACK, LANES), f32)
    far_flat = swap(flat, half)
    far_ints = swap(jnp.concatenate([send_rows, index], axis=1), half)
    flats, indices = [flat], [index]
    for j in range(1, col_size):
        turn = [(i, (i + j) % col_size) for i in range(col_size)]
        flats.append(lax.ppermute(flat, "col", turn))
        indices.append(lax.ppermute(index, "col", turn))
    own, restrict = call(
        functools.partial(prepare_kernel, col_size),
        [shape(rows * PACK + rows, LANES), shape(col_size * CP * B, rows * B)],
        [unpacked, pltpu.VMEM((rows * PACK, LANES), BF16)],
        (*indices, *flats),
        col_size,
        "prepare",
    )
    coupling = call(
        coupling_kernel,
        shape(rows, B, pl.cdiv(span, 2) * LANES),
        [pltpu.VMEM((2, rows, PACK, 2 * LANES), f32)],
        (a_tiles.transpose(1, 0, 2),),
        0,
        "coupling",
    )
    far_flat, far_ints, coupling, own = lax.optimization_barrier((far_flat, far_ints, coupling, own))
    steps = message_order(half)
    self_part, *out = call(
        functools.partial(pack_kernel, n, steps),
        [message(S2)] + [message((3 if has_edge(step) else 2) * S2) for step in steps],
        [unpacked, pltpu.VMEM((2 * rows * PACK, LANES), BF16)]
        + [pltpu.SMEM(x.shape, x.dtype) for x in (send_rows, index, far_ints)]
        + [pltpu.SemaphoreType.DMA((3,))],
        (send_rows, index, far_ints, own, far_flat),
        0,
        "pack",
        3,
    )
    messages = [swap(x, step) for x, step in zip(out, steps)]
    partial = call(
        functools.partial(product_kernel, n, steps),
        shape(col_size * CP * B, CP * B, dtype=f32),
        [
            pltpu.VMEM(((rows + n * S) * B, LANES), BF16),
            pltpu.VMEM((rows * B, CP * B), BF16),
            pltpu.SMEM((span, rows), jnp.int32),
            pltpu.SemaphoreType.DMA((1,)),
        ],
        (neighbors.T, self_part, *messages, own, coupling, restrict),
        0,
        "product",
        1,
    )
    share = col_size * CP * B // n
    parts = lax.all_to_all(
        partial.reshape(n, share, CP * B), "row", split_axis=0, concat_axis=0, tiled=True
    )
    return jnp.sum(parts, axis=0)


def solution(mesh):
    in_specs = (
        P("row", None, None),
        P("row", None),
        P("row", None),
        P("row", "col", None),
        P("row", "col"),
    )
    out_specs = P("row", "col")
    body = functools.partial(shards, mesh.shape["row"], mesh.shape["col"])
    return jax.shard_map(body, mesh=mesh, in_specs=in_specs, out_specs=out_specs, check_vma=False)
```

```python
import functools

import jax
import jax.numpy as jnp
from jax import lax
from jax.experimental import pallas as pl
from jax.experimental.pallas import tpu as pltpu
from jax.sharding import PartitionSpec as P

B = 64
CP = 2
S = 8
S2 = 4
LANES = 128
PACK = B * B // LANES
BF16 = jnp.bfloat16
VMEM = pl.BlockSpec(memory_space=pltpu.VMEM)
SMEM = pl.BlockSpec(memory_space=pltpu.SMEM)
PARAMS = pltpu.CompilerParams(vmem_limit_bytes=40 * 2**20)


def unpack_rows(flat, scratch):
    for l in range(PACK):
        scratch[:, l, :] = flat[:, l * LANES : (l + 1) * LANES].astype(jnp.float32)


def swap_halves(x):
    return jnp.concatenate([x[:, B:], x[:, :B]], axis=1)


def turn_rows(flat, index_of, scratch, out, base):
    rows = scratch.shape[0]
    unpack_rows(flat, scratch)
    for r in range(rows):
        x = scratch[r]
        x = jnp.where(index_of(r) == 0, x, swap_halves(x))
        out[base + r * PACK : base + (r + 1) * PACK, :] = x.astype(BF16)


def mask_row(index, shape):
    lane = lax.broadcasted_iota(jnp.int32, shape, len(shape) - 1)
    return jnp.where((lane >= B) == (index != 0), 1.0, 0.0)


def widen(x, mask):
    return x * mask, swap_halves(x) * mask


def mask_table(index_of, rows):
    sub = lax.broadcasted_iota(jnp.int32, (rows, LANES), 0)
    table = jnp.zeros((rows, LANES), jnp.float32)
    for r in range(rows):
        table = jnp.where(sub == r, mask_row(index_of(r), (rows, LANES)), table)
    return table


def fill(ref, block, table, picks, marks):
    sub = lax.broadcasted_iota(jnp.int32, (marks, LANES), 0)
    mark = jnp.zeros((marks, LANES), jnp.float32)
    for s, (row, index) in enumerate(picks):
        tile = table[pl.ds(pl.multiple_of(row * PACK, PACK), PACK), :]
        ref[(*block, pl.ds(s * PACK, PACK), slice(None))] = tile
        mark = jnp.where(sub == s, mask_row(index, (marks, LANES)), mark)
    ref[(*block, pl.ds(len(picks) * PACK, marks), slice(None))] = mark.astype(BF16)


def alternating(n):
    return [i // 2 + i % 2 * (n // 2) for i in range(n)]


def own_kernel(n, send_ref, index_ref, flat_ref, own_ref, out_ref, left_ref, right_ref, scratch):
    rows = flat_ref.shape[0]
    me = lax.axis_index("row")
    turn_rows(flat_ref, lambda r: index_ref[0, r], scratch, own_ref, 0)
    own_ref[rows * PACK :, :] = mask_table(lambda r: index_ref[0, r], rows).astype(BF16)

    def look(slot):
        row = send_ref[0, slot]
        return row, index_ref[0, row]

    for j, target in enumerate(alternating(n)):
        fill(out_ref, (j,), own_ref, [look(target * S + s) for s in range(S2)], 8)
    for ref, step in ((left_ref, n - 1), (right_ref, 1)):
        first = lax.rem(me + step, n) * S
        fill(ref, (), own_ref, [look(first + s) for s in range(S2, S)], 8)


def coupling_kernel(a_ref, coupling_ref, scratch):
    span, rows, _ = a_ref.shape
    src = lax.broadcasted_iota(jnp.int32, (2 * LANES, 2 * LANES), 0)
    dst = lax.broadcasted_iota(jnp.int32, (2 * LANES, 2 * LANES), 1)
    odd, block, part = dst // LANES, lax.rem(dst // B, 2), lax.rem(dst, B)
    column = jnp.where(part < B // 2, 2 * part, 2 * part - B + 1)
    order = (src == block * LANES + odd * B + column).astype(BF16)
    for pair in range(pl.cdiv(span, 2)):
        blocks = range(2 * pair, min(2 * pair + 2, span))
        buffer = scratch.at[pair % 2]
        for k in blocks:
            unpack_rows(a_ref.at[k], buffer.at[:, :, pl.ds((k % 2) * LANES, LANES)])
        width = len(blocks) * LANES
        packed = buffer[:, :, :width].reshape(rows * PACK, width).astype(BF16)
        ordered = jnp.dot(packed, order[:width], preferred_element_type=jnp.float32).astype(BF16)
        lanes = pl.ds(pair * LANES, LANES)
        coupling_ref[:, :PACK, lanes] = ordered[:, :LANES].reshape(rows, PACK, LANES)
        coupling_ref[:, PACK:, lanes] = ordered[:, LANES:].reshape(rows, PACK, LANES)


def restrict_kernel(rows, col_size, *refs):
    panel_refs, restrict_ref = refs[:col_size], refs[col_size]
    mine = lax.axis_index("col")
    for j, panel_ref in enumerate(panel_refs):
        panel = lax.rem(mine + col_size - j, col_size)
        pieces = []
        for r in range(rows):
            mask = panel_ref[rows * PACK + r : rows * PACK + r + 1, :].astype(jnp.float32)
            x = panel_ref[r * PACK : (r + 1) * PACK, :].astype(jnp.float32)
            pieces.extend(widen(x, mask))
        wide = jnp.concatenate(pieces, axis=0)
        restrict_ref[pl.ds(pl.multiple_of(panel * CP * B, LANES), CP * B), :] = wide.T.astype(BF16)


def product_kernel(
    n, code_ref, ghost_ref, left_ref, right_ref, own_ref, coupling_ref, restrict_ref, out_ref, wide, ap
):
    rows = coupling_ref.shape[0]
    span = code_ref.shape[0]
    me = lax.axis_index("row")

    def place(slot, tile, mask):
        even, odd = widen(tile, mask)
        to = pl.multiple_of(slot * B, B)
        wide[pl.ds(to, PACK), :] = even
        wide[pl.ds(pl.multiple_of(to + PACK, PACK), PACK), :] = odd

    def place_slots(first, ref, block):
        for s in range(S2):
            tile = ref[(*block, pl.ds(s * PACK, PACK), slice(None))]
            place(rows + first + s, tile, ref[(*block, pl.ds(S2 * PACK + s, 1), slice(None))])

    for r in range(rows):
        place(r, own_ref[r * PACK : (r + 1) * PACK, :], own_ref[rows * PACK + r : rows * PACK + r + 1, :])
    for j, source in enumerate(alternating(n)):
        place_slots(source * S, ghost_ref, (j,))
    for ref, step in ((left_ref, n - 1), (right_ref, 1)):
        place_slots(lax.rem(me + step, n) * S + S2, ref, ())

    def row_body(r, carry):
        picked = jnp.concatenate(
            [wide[pl.ds(pl.multiple_of(code_ref[k, r] * B, B), B), :] for k in range(span)], axis=0
        )
        block = jnp.dot(coupling_ref[r, :, : span * B], picked, preferred_element_type=jnp.float32)
        ap[pl.ds(pl.multiple_of(r * B, B), B), :] = block.astype(BF16)
        return carry

    lax.fori_loop(0, rows, row_body, 0, unroll=8)
    coarse = jnp.dot(restrict_ref[...], ap[...], preferred_element_type=jnp.float32)
    share = out_ref.shape[0] // n
    for j, target in enumerate(alternating(n)):
        out_ref[j * share : (j + 1) * share, :] = coarse[target * share : (target + 1) * share]


def shards(n, col_size, a_tiles, neighbors, send_rows, p_tiles, p_index):
    rows, span = a_tiles.shape[0], a_tiles.shape[1]
    flat = p_tiles[:, 0, :]
    index = p_index.T
    f32 = jnp.float32

    def call(body, out_shape, scratch_shapes, operands, smem, name, flops=10**7):
        return pl.pallas_call(
            body,
            out_shape=out_shape,
            in_specs=[SMEM] * smem + [VMEM] * (len(operands) - smem),
            out_specs=jax.tree.map(lambda _: VMEM, out_shape),
            scratch_shapes=scratch_shapes,
            compiler_params=PARAMS,
            cost_estimate=pl.CostEstimate(flops=flops, bytes_accessed=2**20, transcendentals=0),
            name=name,
        )(*operands)

    def shape(*dims, dtype=BF16):
        return jax.ShapeDtypeStruct(dims, dtype)

    def exchange(x):
        return lax.all_to_all(
            x, "row", split_axis=0, concat_axis=0, tiled=True, axis_index_groups=[alternating(n)]
        )

    def ring(x, step):
        return lax.ppermute(x, "row", [(i, (i + step) % n) for i in range(n)])

    unpacked = pltpu.VMEM((rows, PACK, LANES), f32)
    edge = shape(S2 * PACK + 8, LANES)
    blocks = shape(n, S2 * PACK + 8, LANES)
    own, out, left, right = call(
        functools.partial(own_kernel, n),
        [shape(rows * PACK + rows, LANES), blocks, edge, edge],
        [unpacked],
        (send_rows, index, flat),
        2,
        "own",
    )
    out, own, left, right, a_tiles = lax.optimization_barrier((out, own, left, right, a_tiles))
    ghosts = exchange(out)
    from_right, from_left = ring(left, n - 1), ring(right, 1)
    panels = [own] + [
        lax.ppermute(own, "col", [(i, (i + j) % col_size) for i in range(col_size)])
        for j in range(1, col_size)
    ]
    coupling = call(
        coupling_kernel,
        shape(rows, B, pl.cdiv(span, 2) * LANES),
        [pltpu.VMEM((2, rows, PACK, 2 * LANES), f32)],
        (a_tiles.transpose(1, 0, 2),),
        0,
        "coupling",
        2 * 10**9,
    )
    restrict = call(
        functools.partial(restrict_kernel, rows, col_size),
        shape(col_size * CP * B, rows * B),
        [],
        panels,
        0,
        "restrict",
        2 * 10**8,
    )
    partial = call(
        functools.partial(product_kernel, n),
        shape(col_size * CP * B, CP * B, dtype=f32),
        [pltpu.VMEM(((rows + n * S) * B, LANES), BF16), pltpu.VMEM((rows * B, CP * B), BF16)],
        (neighbors.T, ghosts, from_left, from_right, own, coupling, restrict),
        1,
        "product",
        2 * 10**8,
    )
    parts = exchange(partial.reshape(n, col_size * CP * B // n, CP * B))
    return jnp.sum(parts, axis=0)


def solution(mesh):
    in_specs = (
        P("row", None, None),
        P("row", None),
        P("row", None),
        P("row", "col", None),
        P("row", "col"),
    )
    out_specs = P("row", "col")
    body = functools.partial(shards, mesh.shape["row"], mesh.shape["col"])
    return jax.shard_map(body, mesh=mesh, in_specs=in_specs, out_specs=out_specs, check_vma=False)
```

```python
import functools

import jax
import jax.numpy as jnp
from jax import lax
from jax.experimental import pallas as pl
from jax.experimental.pallas import tpu as pltpu
from jax.sharding import PartitionSpec as P

B = 64
CP = 2
S = 8
S2 = 4
LANES = 128
PACK = B * B // LANES
BF16 = jnp.bfloat16
VMEM = pl.BlockSpec(memory_space=pltpu.VMEM)
SMEM = pl.BlockSpec(memory_space=pltpu.SMEM)
HBM = pl.BlockSpec(memory_space=pl.ANY)
WHOLE = 60 * 2**20
PARAMS = pltpu.CompilerParams(vmem_limit_bytes=40 * 2**20)


def unpack_rows(flat, scratch):
    for l in range(PACK):
        scratch[:, l, :] = flat[:, l * LANES : (l + 1) * LANES].astype(jnp.float32)


def swap_halves(x):
    return jnp.concatenate([x[:, B:], x[:, :B]], axis=1)


def turn_rows(index_of, scratch, out, base):
    rows = scratch.shape[0]
    for r in range(rows):
        x = scratch[r]
        x = jnp.where(index_of(r) == 0, x, swap_halves(x))
        out[base + r * PACK : base + (r + 1) * PACK, :] = x.astype(BF16)


def mask_row(index, shape):
    lane = lax.broadcasted_iota(jnp.int32, shape, len(shape) - 1)
    return jnp.where((lane >= B) == (index != 0), 1.0, 0.0)


def widen(x, mask):
    return x * mask, swap_halves(x) * mask


def mask_table(index_of, rows):
    sub = lax.broadcasted_iota(jnp.int32, (rows, LANES), 0)
    table = jnp.zeros((rows, LANES), jnp.float32)
    for r in range(rows):
        table = jnp.where(sub == r, mask_row(index_of(r), (rows, LANES)), table)
    return table


def fill(ref, block, table, picks, marks):
    sub = lax.broadcasted_iota(jnp.int32, (marks, LANES), 0)
    mark = jnp.zeros((marks, LANES), jnp.float32)
    for s, (row, index) in enumerate(picks):
        tile = table[pl.ds(pl.multiple_of(row * PACK, PACK), PACK), :]
        ref[(*block, pl.ds(s * PACK, PACK), slice(None))] = tile
        mark = jnp.where(sub == s, mask_row(index, (marks, LANES)), mark)
    ref[(*block, pl.ds(len(picks) * PACK, marks), slice(None))] = mark.astype(BF16)


def alternating(n):
    return [i // 2 + i % 2 * (n // 2) for i in range(n)]


def own_kernel(n, send_hbm, index_hbm, flat_hbm, out_hbm, own_hbm, left_hbm, right_hbm, *refs):
    send_ref, index_ref, flat_ref, scratch, own_ref, blocks, in_sems, out_sems = refs
    rows = flat_ref.shape[0]
    me = lax.axis_index("row")
    pairs = ((flat_hbm, flat_ref), (send_hbm, send_ref), (index_hbm, index_ref))
    arriving = [pltpu.make_async_copy(x, y, in_sems.at[i]) for i, (x, y) in enumerate(pairs)]
    for copy in arriving:
        copy.start()
    arriving[0].wait()
    unpack_rows(flat_ref, scratch)
    arriving[1].wait()
    arriving[2].wait()
    turn_rows(lambda r: index_ref[0, r], scratch, own_ref, 0)
    own_ref[rows * PACK :, :] = mask_table(lambda r: index_ref[0, r], rows).astype(BF16)
    leaving = [pltpu.make_async_copy(own_ref, own_hbm, out_sems.at[n + 2])]
    leaving[0].start()

    def look(slot):
        row = send_ref[0, slot]
        return row, index_ref[0, row]

    targets = [(target * S, out_hbm.at[j]) for j, target in enumerate(alternating(n))]
    targets.append((lax.rem(me + n - 1, n) * S + S2, left_hbm))
    targets.append((lax.rem(me + 1, n) * S + S2, right_hbm))
    for j, (first, out) in enumerate(targets):
        fill(blocks, (j,), own_ref, [look(first + s) for s in range(S2)], 8)
        leaving.append(pltpu.make_async_copy(blocks.at[j], out, out_sems.at[j]))
        leaving[-1].start()
    for copy in leaving:
        copy.wait()


def coupling_kernel(a_ref, coupling_ref, scratch):
    span, rows, _ = a_ref.shape
    src = lax.broadcasted_iota(jnp.int32, (2 * LANES, 2 * LANES), 0)
    dst = lax.broadcasted_iota(jnp.int32, (2 * LANES, 2 * LANES), 1)
    odd, block, part = dst // LANES, lax.rem(dst // B, 2), lax.rem(dst, B)
    column = jnp.where(part < B // 2, 2 * part, 2 * part - B + 1)
    order = (src == block * LANES + odd * B + column).astype(BF16)
    for pair in range(pl.cdiv(span, 2)):
        blocks = range(2 * pair, min(2 * pair + 2, span))
        buffer = scratch.at[pair % 2]
        for k in blocks:
            unpack_rows(a_ref.at[k], buffer.at[:, :, pl.ds((k % 2) * LANES, LANES)])
        width = len(blocks) * LANES
        packed = buffer[:, :, :width].reshape(rows * PACK, width).astype(BF16)
        ordered = jnp.dot(packed, order[:width], preferred_element_type=jnp.float32).astype(BF16)
        lanes = pl.ds(pair * LANES, LANES)
        coupling_ref[:, :PACK, lanes] = ordered[:, :LANES].reshape(rows, PACK, LANES)
        coupling_ref[:, PACK:, lanes] = ordered[:, LANES:].reshape(rows, PACK, LANES)


def restrict_kernel(rows, col_size, *refs):
    panel_refs, restrict_ref = refs[:col_size], refs[col_size]
    mine = lax.axis_index("col")
    for j, panel_ref in enumerate(panel_refs):
        panel = lax.rem(mine + col_size - j, col_size)
        pieces = []
        for r in range(rows):
            mask = panel_ref[rows * PACK + r : rows * PACK + r + 1, :].astype(jnp.float32)
            x = panel_ref[r * PACK : (r + 1) * PACK, :].astype(jnp.float32)
            pieces.extend(widen(x, mask))
        wide = jnp.concatenate(pieces, axis=0)
        restrict_ref[pl.ds(pl.multiple_of(panel * CP * B, LANES), CP * B), :] = wide.T.astype(BF16)


def product_kernel(
    n, code_ref, ghost_ref, left_ref, right_ref, own_ref, coupling_ref, restrict_ref, out_ref, wide, ap
):
    rows = coupling_ref.shape[0]
    span = code_ref.shape[0]
    me = lax.axis_index("row")

    def place(slot, tile, mask):
        even, odd = widen(tile, mask)
        to = pl.multiple_of(slot * B, B)
        wide[pl.ds(to, PACK), :] = even
        wide[pl.ds(pl.multiple_of(to + PACK, PACK), PACK), :] = odd

    def place_slots(first, ref, block):
        for s in range(S2):
            tile = ref[(*block, pl.ds(s * PACK, PACK), slice(None))]
            place(rows + first + s, tile, ref[(*block, pl.ds(S2 * PACK + s, 1), slice(None))])

    for r in range(rows):
        place(r, own_ref[r * PACK : (r + 1) * PACK, :], own_ref[rows * PACK + r : rows * PACK + r + 1, :])
    for j, source in enumerate(alternating(n)):
        place_slots(source * S, ghost_ref, (j,))
    for ref, step in ((left_ref, n - 1), (right_ref, 1)):
        place_slots(lax.rem(me + step, n) * S + S2, ref, ())

    def row_body(r, carry):
        picked = jnp.concatenate(
            [wide[pl.ds(pl.multiple_of(code_ref[k, r] * B, B), B), :] for k in range(span)], axis=0
        )
        block = jnp.dot(coupling_ref[r, :, : span * B], picked, preferred_element_type=jnp.float32)
        ap[pl.ds(pl.multiple_of(r * B, B), B), :] = block.astype(BF16)
        return carry

    lax.fori_loop(0, rows, row_body, 0, unroll=8)
    coarse = jnp.dot(restrict_ref[...], ap[...], preferred_element_type=jnp.float32)
    share = out_ref.shape[0] // n
    for j, target in enumerate(alternating(n)):
        out_ref[j * share : (j + 1) * share, :] = coarse[target * share : (target + 1) * share]


def shards(n, col_size, a_tiles, neighbors, send_rows, p_tiles, p_index):
    rows, span = a_tiles.shape[0], a_tiles.shape[1]
    flat = p_tiles[:, 0, :]
    index = p_index.T
    f32 = jnp.float32

    def call(body, out_shape, scratch_shapes, operands, smem, name, flops=10**7):
        return pl.pallas_call(
            body,
            out_shape=out_shape,
            in_specs=[SMEM] * smem + [VMEM] * (len(operands) - smem),
            out_specs=jax.tree.map(lambda _: VMEM, out_shape),
            scratch_shapes=scratch_shapes,
            compiler_params=PARAMS,
            cost_estimate=pl.CostEstimate(flops=flops, bytes_accessed=2**20, transcendentals=0),
            name=name,
        )(*operands)

    def shape(*dims, dtype=BF16):
        return jax.ShapeDtypeStruct(dims, dtype)

    def exchange(x):
        return lax.all_to_all(
            x, "row", split_axis=0, concat_axis=0, tiled=True, axis_index_groups=[alternating(n)]
        )

    def ring(x, step):
        return lax.ppermute(x, "row", [(i, (i + step) % n) for i in range(n)])

    unpacked = pltpu.VMEM((rows, PACK, LANES), f32)
    edge = shape(S2 * PACK + 8, LANES)
    blocks = shape(n, S2 * PACK + 8, LANES)
    out, own, left, right = pl.pallas_call(
        functools.partial(own_kernel, n),
        out_shape=(blocks, shape(rows * PACK + rows, LANES), edge, edge),
        in_specs=[HBM] * 3,
        out_specs=(HBM,) * 4,
        scratch_shapes=[
            pltpu.SMEM(send_rows.shape, jnp.int32),
            pltpu.SMEM(index.shape, jnp.int32),
            pltpu.VMEM(flat.shape, BF16),
            unpacked,
            pltpu.VMEM((rows * PACK + rows, LANES), BF16),
            pltpu.VMEM((n + 2, *edge.shape), BF16),
            pltpu.SemaphoreType.DMA((3,)),
            pltpu.SemaphoreType.DMA((n + 3,)),
        ],
        compiler_params=pltpu.CompilerParams(vmem_limit_bytes=WHOLE),
        cost_estimate=pl.CostEstimate(flops=10**7, bytes_accessed=2**20, transcendentals=0),
        name="own",
    )(send_rows, index, flat)
    out, own, left, right, a_tiles = lax.optimization_barrier((out, own, left, right, a_tiles))
    ghosts = exchange(out)
    from_right, from_left = ring(left, n - 1), ring(right, 1)
    panels = [own] + [
        lax.ppermute(own, "col", [(i, (i + j) % col_size) for i in range(col_size)])
        for j in range(1, col_size)
    ]
    coupling = call(
        coupling_kernel,
        shape(rows, B, pl.cdiv(span, 2) * LANES),
        [pltpu.VMEM((2, rows, PACK, 2 * LANES), f32)],
        (a_tiles.transpose(1, 0, 2),),
        0,
        "coupling",
        2 * 10**9,
    )
    restrict = call(
        functools.partial(restrict_kernel, rows, col_size),
        shape(col_size * CP * B, rows * B),
        [],
        panels,
        0,
        "restrict",
        2 * 10**8,
    )
    partial = call(
        functools.partial(product_kernel, n),
        shape(col_size * CP * B, CP * B, dtype=f32),
        [pltpu.VMEM(((rows + n * S) * B, LANES), BF16), pltpu.VMEM((rows * B, CP * B), BF16)],
        (neighbors.T, ghosts, from_left, from_right, own, coupling, restrict),
        1,
        "product",
        2 * 10**8,
    )
    parts = exchange(partial.reshape(n, col_size * CP * B // n, CP * B))
    return jnp.sum(parts, axis=0)


def solution(mesh):
    in_specs = (
        P("row", None, None),
        P("row", None),
        P("row", None),
        P("row", "col", None),
        P("row", "col"),
    )
    out_specs = P("row", "col")
    body = functools.partial(shards, mesh.shape["row"], mesh.shape["col"])
    return jax.shard_map(body, mesh=mesh, in_specs=in_specs, out_specs=out_specs, check_vma=False)
```

```python
import functools

import jax
import jax.numpy as jnp
from jax import lax
from jax.experimental import pallas as pl
from jax.experimental.pallas import tpu as pltpu
from jax.sharding import PartitionSpec as P

B = 64
CP = 2
S = 8
S2 = 4
LANES = 128
PACK = B * B // LANES
BF16 = jnp.bfloat16
VMEM = pl.BlockSpec(memory_space=pltpu.VMEM)
SMEM = pl.BlockSpec(memory_space=pltpu.SMEM)
HBM = pl.BlockSpec(memory_space=pl.ANY)
WHOLE = 60 * 2**20
PARAMS = pltpu.CompilerParams(vmem_limit_bytes=40 * 2**20)


def unpack_rows(flat, scratch):
    for l in range(PACK):
        scratch[:, l, :] = flat[:, l * LANES : (l + 1) * LANES].astype(jnp.float32)


def swap_halves(x):
    return jnp.concatenate([x[:, B:], x[:, :B]], axis=1)


def turn_rows(index_of, scratch, out, base):
    rows = scratch.shape[0]
    for r in range(rows):
        x = scratch[r]
        x = jnp.where(index_of(r) == 0, x, swap_halves(x))
        out[base + r * PACK : base + (r + 1) * PACK, :] = x.astype(BF16)


def mask_row(index, shape):
    lane = lax.broadcasted_iota(jnp.int32, shape, len(shape) - 1)
    return jnp.where((lane >= B) == (index != 0), 1.0, 0.0)


def widen(x, mask):
    return x * mask, swap_halves(x) * mask


def mask_table(index_of, rows):
    sub = lax.broadcasted_iota(jnp.int32, (rows, LANES), 0)
    table = jnp.zeros((rows, LANES), jnp.float32)
    for r in range(rows):
        table = jnp.where(sub == r, mask_row(index_of(r), (rows, LANES)), table)
    return table


def fill(ref, block, table, picks, marks):
    sub = lax.broadcasted_iota(jnp.int32, (marks, LANES), 0)
    mark = jnp.zeros((marks, LANES), jnp.float32)
    for s, (row, index) in enumerate(picks):
        tile = table[pl.ds(pl.multiple_of(row * PACK, PACK), PACK), :]
        ref[(*block, pl.ds(s * PACK, PACK), slice(None))] = tile
        mark = jnp.where(sub == s, mask_row(index, (marks, LANES)), mark)
    ref[(*block, pl.ds(len(picks) * PACK, marks), slice(None))] = mark.astype(BF16)


def alternating(n):
    return [i // 4 + i % 2 * (n // 2) + i // 2 % 2 * (n // 4) for i in range(n)]


def own_kernel(n, send_hbm, index_hbm, flat_hbm, out_hbm, own_hbm, left_hbm, right_hbm, *refs):
    send_ref, index_ref, flat_ref, scratch, own_ref, blocks, in_sems, out_sems = refs
    rows = flat_ref.shape[0]
    me = lax.axis_index("row")
    pairs = ((flat_hbm, flat_ref), (send_hbm, send_ref), (index_hbm, index_ref))
    arriving = [pltpu.make_async_copy(x, y, in_sems.at[i]) for i, (x, y) in enumerate(pairs)]
    for copy in arriving:
        copy.start()
    arriving[0].wait()
    unpack_rows(flat_ref, scratch)
    arriving[1].wait()
    arriving[2].wait()
    turn_rows(lambda r: index_ref[0, r], scratch, own_ref, 0)
    own_ref[rows * PACK :, :] = mask_table(lambda r: index_ref[0, r], rows).astype(BF16)
    leaving = [pltpu.make_async_copy(own_ref, own_hbm, out_sems.at[n + 2])]
    leaving[0].start()

    def look(slot):
        row = send_ref[0, slot]
        return row, index_ref[0, row]

    targets = [(target * S, out_hbm.at[j]) for j, target in enumerate(alternating(n))]
    targets.append((lax.rem(me + n - 1, n) * S + S2, left_hbm))
    targets.append((lax.rem(me + 1, n) * S + S2, right_hbm))
    for j, (first, out) in enumerate(targets):
        fill(blocks, (j,), own_ref, [look(first + s) for s in range(S2)], 8)
        leaving.append(pltpu.make_async_copy(blocks.at[j], out, out_sems.at[j]))
        leaving[-1].start()
    for copy in leaving:
        copy.wait()


def coupling_kernel(a_ref, coupling_ref, scratch):
    span, rows, _ = a_ref.shape
    src = lax.broadcasted_iota(jnp.int32, (2 * LANES, 2 * LANES), 0)
    dst = lax.broadcasted_iota(jnp.int32, (2 * LANES, 2 * LANES), 1)
    odd, block, part = dst // LANES, lax.rem(dst // B, 2), lax.rem(dst, B)
    column = jnp.where(part < B // 2, 2 * part, 2 * part - B + 1)
    order = (src == block * LANES + odd * B + column).astype(BF16)
    for pair in range(pl.cdiv(span, 2)):
        blocks = range(2 * pair, min(2 * pair + 2, span))
        buffer = scratch.at[pair % 2]
        for k in blocks:
            unpack_rows(a_ref.at[k], buffer.at[:, :, pl.ds((k % 2) * LANES, LANES)])
        width = len(blocks) * LANES
        packed = buffer[:, :, :width].reshape(rows * PACK, width).astype(BF16)
        ordered = jnp.dot(packed, order[:width], preferred_element_type=jnp.float32).astype(BF16)
        lanes = pl.ds(pair * LANES, LANES)
        coupling_ref[:, :PACK, lanes] = ordered[:, :LANES].reshape(rows, PACK, LANES)
        coupling_ref[:, PACK:, lanes] = ordered[:, LANES:].reshape(rows, PACK, LANES)


def restrict_kernel(rows, col_size, *refs):
    panel_refs, restrict_ref = refs[:col_size], refs[col_size]
    mine = lax.axis_index("col")
    for j, panel_ref in enumerate(panel_refs):
        panel = lax.rem(mine + col_size - j, col_size)
        pieces = []
        for r in range(rows):
            mask = panel_ref[rows * PACK + r : rows * PACK + r + 1, :].astype(jnp.float32)
            x = panel_ref[r * PACK : (r + 1) * PACK, :].astype(jnp.float32)
            pieces.extend(widen(x, mask))
        wide = jnp.concatenate(pieces, axis=0)
        restrict_ref[pl.ds(pl.multiple_of(panel * CP * B, LANES), CP * B), :] = wide.T.astype(BF16)


def product_kernel(
    n, code_ref, ghost_ref, left_ref, right_ref, own_ref, coupling_ref, restrict_ref, out_ref, wide, ap
):
    rows = coupling_ref.shape[0]
    span = code_ref.shape[0]
    me = lax.axis_index("row")

    def place(slot, tile, mask):
        even, odd = widen(tile, mask)
        to = pl.multiple_of(slot * B, B)
        wide[pl.ds(to, PACK), :] = even
        wide[pl.ds(pl.multiple_of(to + PACK, PACK), PACK), :] = odd

    def place_slots(first, ref, block):
        for s in range(S2):
            tile = ref[(*block, pl.ds(s * PACK, PACK), slice(None))]
            place(rows + first + s, tile, ref[(*block, pl.ds(S2 * PACK + s, 1), slice(None))])

    for r in range(rows):
        place(r, own_ref[r * PACK : (r + 1) * PACK, :], own_ref[rows * PACK + r : rows * PACK + r + 1, :])
    for j, source in enumerate(alternating(n)):
        place_slots(source * S, ghost_ref, (j,))
    for ref, step in ((left_ref, n - 1), (right_ref, 1)):
        place_slots(lax.rem(me + step, n) * S + S2, ref, ())

    def row_body(r, carry):
        picked = jnp.concatenate(
            [wide[pl.ds(pl.multiple_of(code_ref[k, r] * B, B), B), :] for k in range(span)], axis=0
        )
        block = jnp.dot(coupling_ref[r, :, : span * B], picked, preferred_element_type=jnp.float32)
        ap[pl.ds(pl.multiple_of(r * B, B), B), :] = block.astype(BF16)
        return carry

    lax.fori_loop(0, rows, row_body, 0, unroll=8)
    coarse = jnp.dot(restrict_ref[...], ap[...], preferred_element_type=jnp.float32)
    share = out_ref.shape[0] // n
    for j, target in enumerate(alternating(n)):
        out_ref[j * share : (j + 1) * share, :] = coarse[target * share : (target + 1) * share]


def shards(n, col_size, a_tiles, neighbors, send_rows, p_tiles, p_index):
    rows, span = a_tiles.shape[0], a_tiles.shape[1]
    flat = p_tiles[:, 0, :]
    index = p_index.T
    f32 = jnp.float32

    def call(body, out_shape, scratch_shapes, operands, smem, name, flops=10**7):
        return pl.pallas_call(
            body,
            out_shape=out_shape,
            in_specs=[SMEM] * smem + [VMEM] * (len(operands) - smem),
            out_specs=jax.tree.map(lambda _: VMEM, out_shape),
            scratch_shapes=scratch_shapes,
            compiler_params=PARAMS,
            cost_estimate=pl.CostEstimate(flops=flops, bytes_accessed=2**20, transcendentals=0),
            name=name,
        )(*operands)

    def shape(*dims, dtype=BF16):
        return jax.ShapeDtypeStruct(dims, dtype)

    def exchange(x):
        return lax.all_to_all(
            x, "row", split_axis=0, concat_axis=0, tiled=True, axis_index_groups=[alternating(n)]
        )

    def ring(x, step):
        return lax.ppermute(x, "row", [(i, (i + step) % n) for i in range(n)])

    unpacked = pltpu.VMEM((rows, PACK, LANES), f32)
    edge = shape(S2 * PACK + 8, LANES)
    blocks = shape(n, S2 * PACK + 8, LANES)
    out, own, left, right = pl.pallas_call(
        functools.partial(own_kernel, n),
        out_shape=(blocks, shape(rows * PACK + rows, LANES), edge, edge),
        in_specs=[HBM] * 3,
        out_specs=(HBM,) * 4,
        scratch_shapes=[
            pltpu.SMEM(send_rows.shape, jnp.int32),
            pltpu.SMEM(index.shape, jnp.int32),
            pltpu.VMEM(flat.shape, BF16),
            unpacked,
            pltpu.VMEM((rows * PACK + rows, LANES), BF16),
            pltpu.VMEM((n + 2, *edge.shape), BF16),
            pltpu.SemaphoreType.DMA((3,)),
            pltpu.SemaphoreType.DMA((n + 3,)),
        ],
        compiler_params=pltpu.CompilerParams(vmem_limit_bytes=WHOLE),
        cost_estimate=pl.CostEstimate(flops=10**7, bytes_accessed=2**20, transcendentals=0),
        name="own",
    )(send_rows, index, flat)
    out, own, left, right, a_tiles = lax.optimization_barrier((out, own, left, right, a_tiles))
    ghosts = exchange(out)
    from_right, from_left = ring(left, n - 1), ring(right, 1)
    panels = [own] + [
        lax.ppermute(own, "col", [(i, (i + j) % col_size) for i in range(col_size)])
        for j in range(1, col_size)
    ]
    coupling = call(
        coupling_kernel,
        shape(rows, B, pl.cdiv(span, 2) * LANES),
        [pltpu.VMEM((2, rows, PACK, 2 * LANES), f32)],
        (a_tiles.transpose(1, 0, 2),),
        0,
        "coupling",
        2 * 10**9,
    )
    restrict = call(
        functools.partial(restrict_kernel, rows, col_size),
        shape(col_size * CP * B, rows * B),
        [],
        panels,
        0,
        "restrict",
        2 * 10**8,
    )
    partial = call(
        functools.partial(product_kernel, n),
        shape(col_size * CP * B, CP * B, dtype=f32),
        [pltpu.VMEM(((rows + n * S) * B, LANES), BF16), pltpu.VMEM((rows * B, CP * B), BF16)],
        (neighbors.T, ghosts, from_left, from_right, own, coupling, restrict),
        1,
        "product",
        2 * 10**8,
    )
    parts = exchange(partial.reshape(n, col_size * CP * B // n, CP * B))
    return jnp.sum(parts, axis=0)


def solution(mesh):
    in_specs = (
        P("row", None, None),
        P("row", None),
        P("row", None),
        P("row", "col", None),
        P("row", "col"),
    )
    out_specs = P("row", "col")
    body = functools.partial(shards, mesh.shape["row"], mesh.shape["col"])
    return jax.shard_map(body, mesh=mesh, in_specs=in_specs, out_specs=out_specs, check_vma=False)
```

```python
import functools

import jax
import jax.numpy as jnp
from jax import lax
from jax.experimental import pallas as pl
from jax.experimental.pallas import tpu as pltpu
from jax.sharding import PartitionSpec as P

B = 64
CP = 2
S = 8
S2 = 4
LANES = 128
PACK = B * B // LANES
BF16 = jnp.bfloat16
VMEM = pl.BlockSpec(memory_space=pltpu.VMEM)
SMEM = pl.BlockSpec(memory_space=pltpu.SMEM)
HBM = pl.BlockSpec(memory_space=pl.ANY)
WHOLE = 60 * 2**20
PARAMS = pltpu.CompilerParams(vmem_limit_bytes=40 * 2**20)


def unpack_rows(flat, scratch):
    for l in range(PACK):
        scratch[:, l, :] = flat[:, l * LANES : (l + 1) * LANES].astype(jnp.float32)


def swap_halves(x):
    return jnp.concatenate([x[:, B:], x[:, :B]], axis=1)


def turn_rows(index_of, scratch, out, base):
    rows = scratch.shape[0]
    for r in range(rows):
        x = scratch[r]
        x = jnp.where(index_of(r) == 0, x, swap_halves(x))
        out[base + r * PACK : base + (r + 1) * PACK, :] = x.astype(BF16)


def mask_row(index, shape):
    lane = lax.broadcasted_iota(jnp.int32, shape, len(shape) - 1)
    return jnp.where((lane >= B) == (index != 0), 1.0, 0.0)


def widen(x, mask):
    return x * mask, swap_halves(x) * mask


def mask_table(index_of, rows):
    sub = lax.broadcasted_iota(jnp.int32, (rows, LANES), 0)
    table = jnp.zeros((rows, LANES), jnp.float32)
    for r in range(rows):
        table = jnp.where(sub == r, mask_row(index_of(r), (rows, LANES)), table)
    return table


def fill(ref, block, table, picks, marks):
    sub = lax.broadcasted_iota(jnp.int32, (marks, LANES), 0)
    mark = jnp.zeros((marks, LANES), jnp.float32)
    for s, (row, index) in enumerate(picks):
        tile = table[pl.ds(pl.multiple_of(row * PACK, PACK), PACK), :]
        ref[(*block, pl.ds(s * PACK, PACK), slice(None))] = tile
        mark = jnp.where(sub == s, mask_row(index, (marks, LANES)), mark)
    ref[(*block, pl.ds(len(picks) * PACK, marks), slice(None))] = mark.astype(BF16)


def alternating(n):
    return [i // 4 + i % 2 * (n // 2) + i // 2 % 2 * (n // 4) for i in range(n)]


def own_kernel(n, send_hbm, index_hbm, flat_hbm, out_hbm, own_hbm, left_hbm, right_hbm, *refs):
    send_ref, index_ref, flat_ref, scratch, own_ref, blocks, in_sems, out_sems = refs
    rows = flat_ref.shape[0]
    me = lax.axis_index("row")
    pairs = ((flat_hbm, flat_ref), (send_hbm, send_ref), (index_hbm, index_ref))
    arriving = [pltpu.make_async_copy(x, y, in_sems.at[i]) for i, (x, y) in enumerate(pairs)]
    for copy in arriving:
        copy.start()
    arriving[0].wait()
    unpack_rows(flat_ref, scratch)
    arriving[1].wait()
    arriving[2].wait()
    turn_rows(lambda r: index_ref[0, r], scratch, own_ref, 0)
    own_ref[rows * PACK :, :] = mask_table(lambda r: index_ref[0, r], rows).astype(BF16)
    leaving = [pltpu.make_async_copy(own_ref, own_hbm, out_sems.at[n + 2])]
    leaving[0].start()

    def look(slot):
        row = send_ref[0, slot]
        return row, index_ref[0, row]

    targets = [(target * S, out_hbm.at[j]) for j, target in enumerate(alternating(n))]
    targets.append((lax.rem(me + n - 1, n) * S + S2, left_hbm))
    targets.append((lax.rem(me + 1, n) * S + S2, right_hbm))
    for j, (first, out) in enumerate(targets):
        fill(blocks, (j,), own_ref, [look(first + s) for s in range(S2)], 8)
        leaving.append(pltpu.make_async_copy(blocks.at[j], out, out_sems.at[j]))
        leaving[-1].start()
    for copy in leaving:
        copy.wait()


def coupling_kernel(a_ref, coupling_ref, scratch):
    span, rows, _ = a_ref.shape
    src = lax.broadcasted_iota(jnp.int32, (2 * LANES, 2 * LANES), 0)
    dst = lax.broadcasted_iota(jnp.int32, (2 * LANES, 2 * LANES), 1)
    odd, block, part = dst // LANES, lax.rem(dst // B, 2), lax.rem(dst, B)
    column = jnp.where(part < B // 2, 2 * part, 2 * part - B + 1)
    order = (src == block * LANES + odd * B + column).astype(BF16)
    for pair in range(pl.cdiv(span, 2)):
        blocks = range(2 * pair, min(2 * pair + 2, span))
        buffer = scratch.at[pair % 2]
        for k in blocks:
            unpack_rows(a_ref.at[k], buffer.at[:, :, pl.ds((k % 2) * LANES, LANES)])
        width = len(blocks) * LANES
        packed = buffer[:, :, :width].reshape(rows * PACK, width).astype(BF16)
        ordered = jnp.dot(packed, order[:width], preferred_element_type=jnp.float32).astype(BF16)
        lanes = pl.ds(pair * LANES, LANES)
        coupling_ref[:, :PACK, lanes] = ordered[:, :LANES].reshape(rows, PACK, LANES)
        coupling_ref[:, PACK:, lanes] = ordered[:, LANES:].reshape(rows, PACK, LANES)


def restrict_kernel(rows, col_size, *refs):
    panel_refs, restrict_ref = refs[:col_size], refs[col_size]
    mine = lax.axis_index("col")
    for j, panel_ref in enumerate(panel_refs):
        panel = lax.rem(mine + col_size - j, col_size)
        pieces = []
        for r in range(rows):
            mask = panel_ref[rows * PACK + r : rows * PACK + r + 1, :].astype(jnp.float32)
            x = panel_ref[r * PACK : (r + 1) * PACK, :].astype(jnp.float32)
            pieces.extend(widen(x, mask))
        wide = jnp.concatenate(pieces, axis=0)
        restrict_ref[pl.ds(pl.multiple_of(panel * CP * B, LANES), CP * B), :] = wide.T.astype(BF16)


def product_kernel(
    n, code_ref, ghost_ref, left_ref, right_ref, own_ref, coupling_ref, restrict_ref, out_ref, wide, ap
):
    rows = coupling_ref.shape[0]
    span = code_ref.shape[0]
    me = lax.axis_index("row")

    def place(slot, tile, mask):
        even, odd = widen(tile, mask)
        to = pl.multiple_of(slot * B, B)
        wide[pl.ds(to, PACK), :] = even
        wide[pl.ds(pl.multiple_of(to + PACK, PACK), PACK), :] = odd

    def place_slots(first, ref, block):
        for s in range(S2):
            tile = ref[(*block, pl.ds(s * PACK, PACK), slice(None))]
            place(rows + first + s, tile, ref[(*block, pl.ds(S2 * PACK + s, 1), slice(None))])

    for r in range(rows):
        place(r, own_ref[r * PACK : (r + 1) * PACK, :], own_ref[rows * PACK + r : rows * PACK + r + 1, :])
    for j, source in enumerate(alternating(n)):
        place_slots(source * S, ghost_ref, (j,))
    for ref, step in ((left_ref, n - 1), (right_ref, 1)):
        place_slots(lax.rem(me + step, n) * S + S2, ref, ())

    def pair_body(i, carry):
        pair = (2 * i, 2 * i + 1)
        picked = [
            jnp.concatenate(
                [wide[pl.ds(pl.multiple_of(code_ref[k, r] * B, B), B), :] for k in range(span)], axis=0
            )
            for r in pair
        ]
        both = coupling_ref[pl.ds(2 * i, 2), :, : span * B].reshape(2 * B, span * B)
        block = jnp.dot(both, jnp.concatenate(picked, axis=1), preferred_element_type=jnp.float32)
        for h, r in enumerate(pair):
            own = block[h * B : (h + 1) * B, h * LANES : (h + 1) * LANES]
            ap[pl.ds(pl.multiple_of(r * B, B), B), :] = own.astype(BF16)
        return carry

    lax.fori_loop(0, rows // 2, pair_body, 0, unroll=8)
    coarse = jnp.dot(restrict_ref[...], ap[...], preferred_element_type=jnp.float32)
    share = out_ref.shape[0] // n
    for j, target in enumerate(alternating(n)):
        out_ref[j * share : (j + 1) * share, :] = coarse[target * share : (target + 1) * share]


def shards(n, col_size, a_tiles, neighbors, send_rows, p_tiles, p_index):
    rows, span = a_tiles.shape[0], a_tiles.shape[1]
    flat = p_tiles[:, 0, :]
    index = p_index.T
    f32 = jnp.float32

    def call(body, out_shape, scratch_shapes, operands, smem, name, flops=10**7):
        return pl.pallas_call(
            body,
            out_shape=out_shape,
            in_specs=[SMEM] * smem + [VMEM] * (len(operands) - smem),
            out_specs=jax.tree.map(lambda _: VMEM, out_shape),
            scratch_shapes=scratch_shapes,
            compiler_params=PARAMS,
            cost_estimate=pl.CostEstimate(flops=flops, bytes_accessed=2**20, transcendentals=0),
            name=name,
        )(*operands)

    def shape(*dims, dtype=BF16):
        return jax.ShapeDtypeStruct(dims, dtype)

    def exchange(x):
        return lax.all_to_all(
            x, "row", split_axis=0, concat_axis=0, tiled=True, axis_index_groups=[alternating(n)]
        )

    def ring(x, step):
        return lax.ppermute(x, "row", [(i, (i + step) % n) for i in range(n)])

    unpacked = pltpu.VMEM((rows, PACK, LANES), f32)
    edge = shape(S2 * PACK + 8, LANES)
    blocks = shape(n, S2 * PACK + 8, LANES)
    out, own, left, right = pl.pallas_call(
        functools.partial(own_kernel, n),
        out_shape=(blocks, shape(rows * PACK + rows, LANES), edge, edge),
        in_specs=[HBM] * 3,
        out_specs=(HBM,) * 4,
        scratch_shapes=[
            pltpu.SMEM(send_rows.shape, jnp.int32),
            pltpu.SMEM(index.shape, jnp.int32),
            pltpu.VMEM(flat.shape, BF16),
            unpacked,
            pltpu.VMEM((rows * PACK + rows, LANES), BF16),
            pltpu.VMEM((n + 2, *edge.shape), BF16),
            pltpu.SemaphoreType.DMA((3,)),
            pltpu.SemaphoreType.DMA((n + 3,)),
        ],
        compiler_params=pltpu.CompilerParams(vmem_limit_bytes=WHOLE),
        cost_estimate=pl.CostEstimate(flops=10**7, bytes_accessed=2**20, transcendentals=0),
        name="own",
    )(send_rows, index, flat)
    out, own, left, right, a_tiles = lax.optimization_barrier((out, own, left, right, a_tiles))
    ghosts = exchange(out)
    from_right, from_left = ring(left, n - 1), ring(right, 1)
    panels = [own] + [
        lax.ppermute(own, "col", [(i, (i + j) % col_size) for i in range(col_size)])
        for j in range(1, col_size)
    ]
    coupling = call(
        coupling_kernel,
        shape(rows, B, pl.cdiv(span, 2) * LANES),
        [pltpu.VMEM((2, rows, PACK, 2 * LANES), f32)],
        (a_tiles.transpose(1, 0, 2),),
        0,
        "coupling",
        2 * 10**9,
    )
    restrict = call(
        functools.partial(restrict_kernel, rows, col_size),
        shape(col_size * CP * B, rows * B),
        [],
        panels,
        0,
        "restrict",
        2 * 10**8,
    )
    partial = call(
        functools.partial(product_kernel, n),
        shape(col_size * CP * B, CP * B, dtype=f32),
        [pltpu.VMEM(((rows + n * S) * B, LANES), BF16), pltpu.VMEM((rows * B, CP * B), BF16)],
        (neighbors.T, ghosts, from_left, from_right, own, coupling, restrict),
        1,
        "product",
        2 * 10**8,
    )
    parts = exchange(partial.reshape(n, col_size * CP * B // n, CP * B))
    return jnp.sum(parts, axis=0)


def solution(mesh):
    in_specs = (
        P("row", None, None),
        P("row", None),
        P("row", None),
        P("row", "col", None),
        P("row", "col"),
    )
    out_specs = P("row", "col")
    body = functools.partial(shards, mesh.shape["row"], mesh.shape["col"])
    return jax.shard_map(body, mesh=mesh, in_specs=in_specs, out_specs=out_specs, check_vma=False)
```

```python
import functools

import jax
import jax.numpy as jnp
from jax import lax
from jax.experimental import pallas as pl
from jax.experimental.pallas import tpu as pltpu
from jax.sharding import PartitionSpec as P

B = 64
CP = 2
S = 8
S2 = 4
LANES = 128
PACK = B * B // LANES
BF16 = jnp.bfloat16
VMEM = pl.BlockSpec(memory_space=pltpu.VMEM)
SMEM = pl.BlockSpec(memory_space=pltpu.SMEM)
HBM = pl.BlockSpec(memory_space=pl.ANY)
WHOLE = 60 * 2**20
PARAMS = pltpu.CompilerParams(vmem_limit_bytes=40 * 2**20)


def unpack_rows(flat, scratch):
    for l in range(PACK):
        scratch[:, l, :] = flat[:, l * LANES : (l + 1) * LANES].astype(jnp.float32)


def swap_halves(x):
    return jnp.concatenate([x[:, B:], x[:, :B]], axis=1)


def turn_rows(index_of, scratch, out, base):
    rows = scratch.shape[0]
    for r in range(rows):
        x = scratch[r]
        x = jnp.where(index_of(r) == 0, x, swap_halves(x))
        out[base + r * PACK : base + (r + 1) * PACK, :] = x.astype(BF16)


def mask_row(index, shape):
    lane = lax.broadcasted_iota(jnp.int32, shape, len(shape) - 1)
    return jnp.where((lane >= B) == (index != 0), 1.0, 0.0)


def widen(x, mask):
    return x * mask, swap_halves(x) * mask


def mask_table(index_of, rows):
    sub = lax.broadcasted_iota(jnp.int32, (rows, LANES), 0)
    table = jnp.zeros((rows, LANES), jnp.float32)
    for r in range(rows):
        table = jnp.where(sub == r, mask_row(index_of(r), (rows, LANES)), table)
    return table


def alternating(n):
    return [i // 4 + i % 2 * (n // 2) + i // 2 % 2 * (n // 4) for i in range(n)]


def own_kernel(n, send_hbm, index_hbm, flat_hbm, out_hbm, own_hbm, left_hbm, right_hbm, *refs):
    send_ref, index_ref, flat_ref, scratch, own_ref, blocks, in_sems, out_sems = refs
    rows = flat_ref.shape[0]
    me = lax.axis_index("row")
    pairs = ((flat_hbm, flat_ref), (send_hbm, send_ref), (index_hbm, index_ref))
    arriving = [pltpu.make_async_copy(x, y, in_sems.at[i]) for i, (x, y) in enumerate(pairs)]
    for copy in arriving:
        copy.start()
    arriving[1].wait()
    arriving[2].wait()
    targets = [(target * S, out_hbm.at[j]) for j, target in enumerate(alternating(n))]
    targets.append((lax.rem(me + n - 1, n) * S + S2, left_hbm))
    targets.append((lax.rem(me + 1, n) * S + S2, right_hbm))
    picks = [[send_ref[0, first + s] for s in range(S2)] for first, _ in targets]
    sub = lax.broadcasted_iota(jnp.int32, (8, LANES), 0)
    for j, picked in enumerate(picks):
        mark = jnp.zeros((8, LANES), jnp.float32)
        for s, row in enumerate(picked):
            mark = jnp.where(sub == s, mask_row(index_ref[0, row], (8, LANES)), mark)
        blocks[j, S2 * PACK :, :] = mark.astype(BF16)
    own_ref[rows * PACK :, :] = mask_table(lambda r: index_ref[0, r], rows).astype(BF16)
    arriving[0].wait()
    unpack_rows(flat_ref, scratch)
    turn_rows(lambda r: index_ref[0, r], scratch, own_ref, 0)
    leaving = [pltpu.make_async_copy(own_ref, own_hbm, out_sems.at[n + 2])]
    leaving[0].start()
    for j, (picked, (_, out)) in enumerate(zip(picks, targets)):
        for s, row in enumerate(picked):
            tile = own_ref[pl.ds(pl.multiple_of(row * PACK, PACK), PACK), :]
            blocks[j, s * PACK : (s + 1) * PACK, :] = tile
        leaving.append(pltpu.make_async_copy(blocks.at[j], out, out_sems.at[j]))
        leaving[-1].start()
    for copy in leaving:
        copy.wait()


def coupling_kernel(a_ref, coupling_ref, scratch):
    span, rows, _ = a_ref.shape
    src = lax.broadcasted_iota(jnp.int32, (2 * LANES, 2 * LANES), 0)
    dst = lax.broadcasted_iota(jnp.int32, (2 * LANES, 2 * LANES), 1)
    odd, block, part = dst // LANES, lax.rem(dst // B, 2), lax.rem(dst, B)
    column = jnp.where(part < B // 2, 2 * part, 2 * part - B + 1)
    order = (src == block * LANES + odd * B + column).astype(BF16)
    for pair in range(pl.cdiv(span, 2)):
        blocks = range(2 * pair, min(2 * pair + 2, span))
        buffer = scratch.at[pair % 2]
        for k in blocks:
            unpack_rows(a_ref.at[k], buffer.at[:, :, pl.ds((k % 2) * LANES, LANES)])
        width = len(blocks) * LANES
        packed = buffer[:, :, :width].reshape(rows * PACK, width).astype(BF16)
        ordered = jnp.dot(packed, order[:width], preferred_element_type=jnp.float32).astype(BF16)
        lanes = pl.ds(pair * LANES, LANES)
        coupling_ref[:, :PACK, lanes] = ordered[:, :LANES].reshape(rows, PACK, LANES)
        coupling_ref[:, PACK:, lanes] = ordered[:, LANES:].reshape(rows, PACK, LANES)


def restrict_kernel(rows, col_size, *refs):
    panel_refs, restrict_ref = refs[:col_size], refs[col_size]
    mine = lax.axis_index("col")
    for j, panel_ref in enumerate(panel_refs):
        panel = lax.rem(mine + col_size - j, col_size)
        pieces = []
        for r in range(rows):
            mask = panel_ref[rows * PACK + r : rows * PACK + r + 1, :].astype(jnp.float32)
            x = panel_ref[r * PACK : (r + 1) * PACK, :].astype(jnp.float32)
            pieces.extend(widen(x, mask))
        wide = jnp.concatenate(pieces, axis=0)
        restrict_ref[pl.ds(pl.multiple_of(panel * CP * B, LANES), CP * B), :] = wide.T.astype(BF16)


def product_kernel(
    n, code_ref, ghost_ref, left_ref, right_ref, own_ref, coupling_ref, restrict_ref, out_ref, wide, ap
):
    rows = coupling_ref.shape[0]
    span = code_ref.shape[0]
    me = lax.axis_index("row")

    def place(slot, tile, mask):
        even, odd = widen(tile, mask)
        to = pl.multiple_of(slot * B, B)
        wide[pl.ds(to, PACK), :] = even
        wide[pl.ds(pl.multiple_of(to + PACK, PACK), PACK), :] = odd

    def place_slots(first, ref, block):
        for s in range(S2):
            tile = ref[(*block, pl.ds(s * PACK, PACK), slice(None))]
            place(rows + first + s, tile, ref[(*block, pl.ds(S2 * PACK + s, 1), slice(None))])

    for r in range(rows):
        place(r, own_ref[r * PACK : (r + 1) * PACK, :], own_ref[rows * PACK + r : rows * PACK + r + 1, :])
    for j, source in enumerate(alternating(n)):
        place_slots(source * S, ghost_ref, (j,))
    for ref, step in ((left_ref, n - 1), (right_ref, 1)):
        place_slots(lax.rem(me + step, n) * S + S2, ref, ())

    def pair_body(i, carry):
        pair = (2 * i, 2 * i + 1)
        picked = [
            jnp.concatenate(
                [wide[pl.ds(pl.multiple_of(code_ref[k, r] * B, B), B), :] for k in range(span)], axis=0
            )
            for r in pair
        ]
        both = coupling_ref[pl.ds(2 * i, 2), :, : span * B].reshape(2 * B, span * B)
        block = jnp.dot(both, jnp.concatenate(picked, axis=1), preferred_element_type=jnp.float32)
        for h, r in enumerate(pair):
            own = block[h * B : (h + 1) * B, h * LANES : (h + 1) * LANES]
            ap[pl.ds(pl.multiple_of(r * B, B), B), :] = own.astype(BF16)
        return carry

    lax.fori_loop(0, rows // 2, pair_body, 0, unroll=8)
    coarse = jnp.dot(restrict_ref[...], ap[...], preferred_element_type=jnp.float32)
    share = out_ref.shape[0] // n
    for j, target in enumerate(alternating(n)):
        out_ref[j * share : (j + 1) * share, :] = coarse[target * share : (target + 1) * share]


def shards(n, col_size, a_tiles, neighbors, send_rows, p_tiles, p_index):
    rows, span = a_tiles.shape[0], a_tiles.shape[1]
    flat = p_tiles[:, 0, :]
    index = p_index.T
    f32 = jnp.float32

    def call(body, out_shape, scratch_shapes, operands, smem, name, flops=10**7):
        return pl.pallas_call(
            body,
            out_shape=out_shape,
            in_specs=[SMEM] * smem + [VMEM] * (len(operands) - smem),
            out_specs=jax.tree.map(lambda _: VMEM, out_shape),
            scratch_shapes=scratch_shapes,
            compiler_params=PARAMS,
            cost_estimate=pl.CostEstimate(flops=flops, bytes_accessed=2**20, transcendentals=0),
            name=name,
        )(*operands)

    def shape(*dims, dtype=BF16):
        return jax.ShapeDtypeStruct(dims, dtype)

    def exchange(x):
        return lax.all_to_all(
            x, "row", split_axis=0, concat_axis=0, tiled=True, axis_index_groups=[alternating(n)]
        )

    def ring(x, step):
        return lax.ppermute(x, "row", [(i, (i + step) % n) for i in range(n)])

    unpacked = pltpu.VMEM((rows, PACK, LANES), f32)
    edge = shape(S2 * PACK + 8, LANES)
    blocks = shape(n, S2 * PACK + 8, LANES)
    out, own, left, right = pl.pallas_call(
        functools.partial(own_kernel, n),
        out_shape=(blocks, shape(rows * PACK + rows, LANES), edge, edge),
        in_specs=[HBM] * 3,
        out_specs=(HBM,) * 4,
        scratch_shapes=[
            pltpu.SMEM(send_rows.shape, jnp.int32),
            pltpu.SMEM(index.shape, jnp.int32),
            pltpu.VMEM(flat.shape, BF16),
            unpacked,
            pltpu.VMEM((rows * PACK + rows, LANES), BF16),
            pltpu.VMEM((n + 2, *edge.shape), BF16),
            pltpu.SemaphoreType.DMA((3,)),
            pltpu.SemaphoreType.DMA((n + 3,)),
        ],
        compiler_params=pltpu.CompilerParams(vmem_limit_bytes=WHOLE),
        cost_estimate=pl.CostEstimate(flops=10**7, bytes_accessed=2**20, transcendentals=0),
        name="own",
    )(send_rows, index, flat)
    out, own, left, right, a_tiles = lax.optimization_barrier((out, own, left, right, a_tiles))
    ghosts = exchange(out)
    from_right, from_left = ring(left, n - 1), ring(right, 1)
    panels = [own] + [
        lax.ppermute(own, "col", [(i, (i + j) % col_size) for i in range(col_size)])
        for j in range(1, col_size)
    ]
    coupling = call(
        coupling_kernel,
        shape(rows, B, pl.cdiv(span, 2) * LANES),
        [pltpu.VMEM((2, rows, PACK, 2 * LANES), f32)],
        (a_tiles.transpose(1, 0, 2),),
        0,
        "coupling",
        2 * 10**9,
    )
    restrict = call(
        functools.partial(restrict_kernel, rows, col_size),
        shape(col_size * CP * B, rows * B),
        [],
        panels,
        0,
        "restrict",
        2 * 10**8,
    )
    partial = call(
        functools.partial(product_kernel, n),
        shape(col_size * CP * B, CP * B, dtype=f32),
        [pltpu.VMEM(((rows + n * S) * B, LANES), BF16), pltpu.VMEM((rows * B, CP * B), BF16)],
        (neighbors.T, ghosts, from_left, from_right, own, coupling, restrict),
        1,
        "product",
        2 * 10**8,
    )
    parts = exchange(partial.reshape(n, col_size * CP * B // n, CP * B))
    return jnp.sum(parts, axis=0)


def solution(mesh):
    in_specs = (
        P("row", None, None),
        P("row", None),
        P("row", None),
        P("row", "col", None),
        P("row", "col"),
    )
    out_specs = P("row", "col")
    body = functools.partial(shards, mesh.shape["row"], mesh.shape["col"])
    return jax.shard_map(body, mesh=mesh, in_specs=in_specs, out_specs=out_specs, check_vma=False)
```

```python
import functools

import jax
import jax.numpy as jnp
from jax import lax
from jax.experimental import pallas as pl
from jax.experimental.pallas import tpu as pltpu
from jax.sharding import PartitionSpec as P

B = 64
CP = 2
S = 8
S2 = 4
LANES = 128
PACK = B * B // LANES
BF16 = jnp.bfloat16
VMEM = pl.BlockSpec(memory_space=pltpu.VMEM)
SMEM = pl.BlockSpec(memory_space=pltpu.SMEM)
HBM = pl.BlockSpec(memory_space=pl.ANY)
WHOLE = 60 * 2**20
PARAMS = pltpu.CompilerParams(vmem_limit_bytes=40 * 2**20)


def unpack_rows(flat, scratch):
    for l in range(PACK):
        scratch[:, l, :] = flat[:, l * LANES : (l + 1) * LANES].astype(jnp.float32)


def swap_halves(x):
    return jnp.concatenate([x[:, B:], x[:, :B]], axis=1)


def turn_rows(index_of, scratch, out, base):
    rows = scratch.shape[0]
    for r in range(rows):
        x = scratch[r]
        x = jnp.where(index_of(r) == 0, x, swap_halves(x))
        out[base + r * PACK : base + (r + 1) * PACK, :] = x.astype(BF16)


def mask_row(index, shape):
    lane = lax.broadcasted_iota(jnp.int32, shape, len(shape) - 1)
    return jnp.where((lane >= B) == (index != 0), 1.0, 0.0)


def widen(x, mask):
    return x * mask, swap_halves(x) * mask


def mask_table(index_of, rows):
    sub = lax.broadcasted_iota(jnp.int32, (rows, LANES), 0)
    table = jnp.zeros((rows, LANES), jnp.float32)
    for r in range(rows):
        table = jnp.where(sub == r, mask_row(index_of(r), (rows, LANES)), table)
    return table


def fill(ref, block, table, picks, marks):
    sub = lax.broadcasted_iota(jnp.int32, (marks, LANES), 0)
    mark = jnp.zeros((marks, LANES), jnp.float32)
    for s, (row, index) in enumerate(picks):
        tile = table[pl.ds(pl.multiple_of(row * PACK, PACK), PACK), :]
        ref[(*block, pl.ds(s * PACK, PACK), slice(None))] = tile
        mark = jnp.where(sub == s, mask_row(index, (marks, LANES)), mark)
    ref[(*block, pl.ds(len(picks) * PACK, marks), slice(None))] = mark.astype(BF16)


def alternating(n):
    return [i // 4 + i % 2 * (n // 2) + i // 2 % 2 * (n // 4) for i in range(n)]


def own_kernel(n, send_hbm, index_hbm, flat_hbm, out_ref, own_ref, left_ref, right_ref, *refs):
    send_ref, index_ref, flat_ref, scratch, sems = refs
    rows = flat_ref.shape[0]
    me = lax.axis_index("row")
    pairs = ((flat_hbm, flat_ref), (send_hbm, send_ref), (index_hbm, index_ref))
    copies = [pltpu.make_async_copy(x, y, sems.at[i]) for i, (x, y) in enumerate(pairs)]
    for copy in copies:
        copy.start()
    for copy in copies:
        copy.wait()
    unpack_rows(flat_ref, scratch)
    turn_rows(lambda r: index_ref[0, r], scratch, own_ref, 0)
    own_ref[rows * PACK :, :] = mask_table(lambda r: index_ref[0, r], rows).astype(BF16)

    def look(slot):
        row = send_ref[0, slot]
        return row, index_ref[0, row]

    for j, target in enumerate(alternating(n)):
        fill(out_ref, (j,), own_ref, [look(target * S + s) for s in range(S2)], 8)
    for ref, step in ((left_ref, n - 1), (right_ref, 1)):
        first = lax.rem(me + step, n) * S
        fill(ref, (), own_ref, [look(first + s) for s in range(S2, S)], 8)


def coupling_kernel(a_ref, coupling_ref, scratch):
    span, rows, _ = a_ref.shape
    src = lax.broadcasted_iota(jnp.int32, (2 * LANES, 2 * LANES), 0)
    dst = lax.broadcasted_iota(jnp.int32, (2 * LANES, 2 * LANES), 1)
    odd, block, part = dst // LANES, lax.rem(dst // B, 2), lax.rem(dst, B)
    column = jnp.where(part < B // 2, 2 * part, 2 * part - B + 1)
    order = (src == block * LANES + odd * B + column).astype(BF16)
    for pair in range(pl.cdiv(span, 2)):
        blocks = range(2 * pair, min(2 * pair + 2, span))
        buffer = scratch.at[pair % 2]
        for k in blocks:
            unpack_rows(a_ref.at[k], buffer.at[:, :, pl.ds((k % 2) * LANES, LANES)])
        width = len(blocks) * LANES
        packed = buffer[:, :, :width].reshape(rows * PACK, width).astype(BF16)
        ordered = jnp.dot(packed, order[:width], preferred_element_type=jnp.float32).astype(BF16)
        lanes = pl.ds(pair * LANES, LANES)
        coupling_ref[:, :PACK, lanes] = ordered[:, :LANES].reshape(rows, PACK, LANES)
        coupling_ref[:, PACK:, lanes] = ordered[:, LANES:].reshape(rows, PACK, LANES)


def restrict_kernel(rows, col_size, *refs):
    panel_refs, restrict_ref = refs[:col_size], refs[col_size]
    mine = lax.axis_index("col")
    for j, panel_ref in enumerate(panel_refs):
        panel = lax.rem(mine + col_size - j, col_size)
        pieces = []
        for r in range(rows):
            mask = panel_ref[rows * PACK + r : rows * PACK + r + 1, :].astype(jnp.float32)
            x = panel_ref[r * PACK : (r + 1) * PACK, :].astype(jnp.float32)
            pieces.extend(widen(x, mask))
        wide = jnp.concatenate(pieces, axis=0)
        restrict_ref[pl.ds(pl.multiple_of(panel * CP * B, LANES), CP * B), :] = wide.T.astype(BF16)


def product_kernel(
    n, code_ref, ghost_ref, left_ref, right_ref, own_ref, coupling_ref, restrict_ref, out_ref, wide, ap
):
    rows = coupling_ref.shape[0]
    span = code_ref.shape[0]
    me = lax.axis_index("row")

    def place(slot, tile, mask):
        even, odd = widen(tile, mask)
        to = pl.multiple_of(slot * B, B)
        wide[pl.ds(to, PACK), :] = even
        wide[pl.ds(pl.multiple_of(to + PACK, PACK), PACK), :] = odd

    def place_slots(first, ref, block):
        for s in range(S2):
            tile = ref[(*block, pl.ds(s * PACK, PACK), slice(None))]
            place(rows + first + s, tile, ref[(*block, pl.ds(S2 * PACK + s, 1), slice(None))])

    for r in range(rows):
        place(r, own_ref[r * PACK : (r + 1) * PACK, :], own_ref[rows * PACK + r : rows * PACK + r + 1, :])
    for j, source in enumerate(alternating(n)):
        place_slots(source * S, ghost_ref, (j,))
    for ref, step in ((left_ref, n - 1), (right_ref, 1)):
        place_slots(lax.rem(me + step, n) * S + S2, ref, ())

    def pair_body(i, carry):
        pair = (2 * i, 2 * i + 1)
        picked = [
            jnp.concatenate(
                [wide[pl.ds(pl.multiple_of(code_ref[k, r] * B, B), B), :] for k in range(span)], axis=0
            )
            for r in pair
        ]
        both = coupling_ref[pl.ds(2 * i, 2), :, : span * B].reshape(2 * B, span * B)
        block = jnp.dot(both, jnp.concatenate(picked, axis=1), preferred_element_type=jnp.float32)
        for h, r in enumerate(pair):
            own = block[h * B : (h + 1) * B, h * LANES : (h + 1) * LANES]
            ap[pl.ds(pl.multiple_of(r * B, B), B), :] = own.astype(BF16)
        return carry

    lax.fori_loop(0, rows // 2, pair_body, 0, unroll=8)
    coarse = jnp.dot(restrict_ref[...], ap[...], preferred_element_type=jnp.float32)
    share = out_ref.shape[0] // n
    for j, target in enumerate(alternating(n)):
        out_ref[j * share : (j + 1) * share, :] = coarse[target * share : (target + 1) * share]


def shards(n, col_size, a_tiles, neighbors, send_rows, p_tiles, p_index):
    rows, span = a_tiles.shape[0], a_tiles.shape[1]
    flat = p_tiles[:, 0, :]
    index = p_index.T
    f32 = jnp.float32

    def call(body, out_shape, scratch_shapes, operands, smem, name, flops=10**7):
        return pl.pallas_call(
            body,
            out_shape=out_shape,
            in_specs=[SMEM] * smem + [VMEM] * (len(operands) - smem),
            out_specs=jax.tree.map(lambda _: VMEM, out_shape),
            scratch_shapes=scratch_shapes,
            compiler_params=PARAMS,
            cost_estimate=pl.CostEstimate(flops=flops, bytes_accessed=2**20, transcendentals=0),
            name=name,
        )(*operands)

    def shape(*dims, dtype=BF16):
        return jax.ShapeDtypeStruct(dims, dtype)

    def exchange(x):
        return lax.all_to_all(
            x, "row", split_axis=0, concat_axis=0, tiled=True, axis_index_groups=[alternating(n)]
        )

    def ring(x, step):
        return lax.ppermute(x, "row", [(i, (i + step) % n) for i in range(n)])

    unpacked = pltpu.VMEM((rows, PACK, LANES), f32)
    edge = shape(S2 * PACK + 8, LANES)
    blocks = shape(n, S2 * PACK + 8, LANES)
    out, own, left, right = pl.pallas_call(
        functools.partial(own_kernel, n),
        out_shape=(blocks, shape(rows * PACK + rows, LANES), edge, edge),
        in_specs=[HBM] * 3,
        out_specs=(VMEM,) * 4,
        scratch_shapes=[
            pltpu.SMEM(send_rows.shape, jnp.int32),
            pltpu.SMEM(index.shape, jnp.int32),
            pltpu.VMEM(flat.shape, BF16),
            unpacked,
            pltpu.SemaphoreType.DMA((3,)),
        ],
        compiler_params=pltpu.CompilerParams(vmem_limit_bytes=WHOLE),
        cost_estimate=pl.CostEstimate(flops=10**7, bytes_accessed=2**20, transcendentals=0),
        name="own",
    )(send_rows, index, flat)
    out, own, left, right, a_tiles = lax.optimization_barrier((out, own, left, right, a_tiles))
    ghosts = exchange(out)
    from_right, from_left = ring(left, n - 1), ring(right, 1)
    panels = [own] + [
        lax.ppermute(own, "col", [(i, (i + j) % col_size) for i in range(col_size)])
        for j in range(1, col_size)
    ]
    coupling = call(
        coupling_kernel,
        shape(rows, B, pl.cdiv(span, 2) * LANES),
        [pltpu.VMEM((2, rows, PACK, 2 * LANES), f32)],
        (a_tiles.transpose(1, 0, 2),),
        0,
        "coupling",
        2 * 10**9,
    )
    restrict = call(
        functools.partial(restrict_kernel, rows, col_size),
        shape(col_size * CP * B, rows * B),
        [],
        panels,
        0,
        "restrict",
        2 * 10**8,
    )
    partial = call(
        functools.partial(product_kernel, n),
        shape(col_size * CP * B, CP * B, dtype=f32),
        [pltpu.VMEM(((rows + n * S) * B, LANES), BF16), pltpu.VMEM((rows * B, CP * B), BF16)],
        (neighbors.T, ghosts, from_left, from_right, own, coupling, restrict),
        1,
        "product",
        2 * 10**8,
    )
    parts = exchange(partial.reshape(n, col_size * CP * B // n, CP * B))
    return jnp.sum(parts, axis=0)


def solution(mesh):
    in_specs = (
        P("row", None, None),
        P("row", None),
        P("row", None),
        P("row", "col", None),
        P("row", "col"),
    )
    out_specs = P("row", "col")
    body = functools.partial(shards, mesh.shape["row"], mesh.shape["col"])
    return jax.shard_map(body, mesh=mesh, in_specs=in_specs, out_specs=out_specs, check_vma=False)
```

```python
import functools

import jax
import jax.numpy as jnp
from jax import lax
from jax.experimental import pallas as pl
from jax.experimental.pallas import tpu as pltpu
from jax.sharding import PartitionSpec as P

B = 64
CP = 2
S = 8
S2 = 4
LANES = 128
PACK = B * B // LANES
BF16 = jnp.bfloat16
VMEM = pl.BlockSpec(memory_space=pltpu.VMEM)
SMEM = pl.BlockSpec(memory_space=pltpu.SMEM)
HBM = pl.BlockSpec(memory_space=pl.ANY)
WHOLE = 60 * 2**20
PARAMS = pltpu.CompilerParams(vmem_limit_bytes=40 * 2**20)


def unpack_rows(flat, scratch):
    for l in range(PACK):
        scratch[:, l, :] = flat[:, l * LANES : (l + 1) * LANES].astype(jnp.float32)


def swap_halves(x):
    return jnp.concatenate([x[:, B:], x[:, :B]], axis=1)


def turn_rows(index_of, scratch, out, base):
    rows = scratch.shape[0]
    for r in range(rows):
        x = scratch[r]
        x = jnp.where(index_of(r) == 0, x, swap_halves(x))
        out[base + r * PACK : base + (r + 1) * PACK, :] = x.astype(BF16)


def mask_row(index, shape):
    lane = lax.broadcasted_iota(jnp.int32, shape, len(shape) - 1)
    return jnp.where((lane >= B) == (index != 0), 1.0, 0.0)


def widen(x, mask):
    return x * mask, swap_halves(x) * mask


def mask_table(index_of, rows):
    sub = lax.broadcasted_iota(jnp.int32, (rows, LANES), 0)
    table = jnp.zeros((rows, LANES), jnp.float32)
    for r in range(rows):
        table = jnp.where(sub == r, mask_row(index_of(r), (rows, LANES)), table)
    return table


def fill(ref, block, table, picks, marks):
    sub = lax.broadcasted_iota(jnp.int32, (marks, LANES), 0)
    mark = jnp.zeros((marks, LANES), jnp.float32)
    for s, (row, index) in enumerate(picks):
        tile = table[pl.ds(pl.multiple_of(row * PACK, PACK), PACK), :]
        ref[(*block, pl.ds(s * PACK, PACK), slice(None))] = tile
        mark = jnp.where(sub == s, mask_row(index, (marks, LANES)), mark)
    ref[(*block, pl.ds(len(picks) * PACK, marks), slice(None))] = mark.astype(BF16)


def alternating(n):
    return [i // 4 + i % 2 * (n // 2) + i // 2 % 2 * (n // 4) for i in range(n)]


def own_kernel(n, send_hbm, index_hbm, flat_hbm, out_ref, own_ref, left_ref, right_ref, *refs):
    send_ref, index_ref, flat_ref, scratch, sems = refs
    rows = flat_ref.shape[0]
    me = lax.axis_index("row")
    pairs = ((flat_hbm, flat_ref), (send_hbm, send_ref), (index_hbm, index_ref))
    copies = [pltpu.make_async_copy(x, y, sems.at[i]) for i, (x, y) in enumerate(pairs)]
    for copy in copies:
        copy.start()
    for copy in copies:
        copy.wait()
    unpack_rows(flat_ref, scratch)
    turn_rows(lambda r: index_ref[0, r], scratch, own_ref, 0)
    own_ref[rows * PACK :, :] = mask_table(lambda r: index_ref[0, r], rows).astype(BF16)

    def look(slot):
        row = send_ref[0, slot]
        return row, index_ref[0, row]

    for j, target in enumerate(alternating(n)):
        fill(out_ref, (j,), own_ref, [look(target * S + s) for s in range(S2)], 8)
    for ref, step in ((left_ref, n - 1), (right_ref, 1)):
        first = lax.rem(me + step, n) * S
        fill(ref, (), own_ref, [look(first + s) for s in range(S2, S)], 8)


def coupling_kernel(a_ref, coupling_ref, scratch):
    span, rows, _ = a_ref.shape
    src = lax.broadcasted_iota(jnp.int32, (2 * LANES, 2 * LANES), 0)
    dst = lax.broadcasted_iota(jnp.int32, (2 * LANES, 2 * LANES), 1)
    odd, block, part = dst // LANES, lax.rem(dst // B, 2), lax.rem(dst, B)
    column = jnp.where(part < B // 2, 2 * part, 2 * part - B + 1)
    order = (src == block * LANES + odd * B + column).astype(BF16)
    for pair in range(pl.cdiv(span, 2)):
        blocks = range(2 * pair, min(2 * pair + 2, span))
        buffer = scratch.at[pair % 2]
        for k in blocks:
            unpack_rows(a_ref.at[k], buffer.at[:, :, pl.ds((k % 2) * LANES, LANES)])
        width = len(blocks) * LANES
        packed = buffer[:, :, :width].reshape(rows * PACK, width).astype(BF16)
        ordered = jnp.dot(packed, order[:width], preferred_element_type=jnp.float32).astype(BF16)
        lanes = pl.ds(pair * LANES, LANES)
        coupling_ref[:, :PACK, lanes] = ordered[:, :LANES].reshape(rows, PACK, LANES)
        coupling_ref[:, PACK:, lanes] = ordered[:, LANES:].reshape(rows, PACK, LANES)


def restrict_kernel(rows, col_size, *refs):
    panel_refs, restrict_ref = refs[:col_size], refs[col_size]
    mine = lax.axis_index("col")
    for j, panel_ref in enumerate(panel_refs):
        panel = lax.rem(mine + col_size - j, col_size)
        pieces = []
        for r in range(rows):
            mask = panel_ref[rows * PACK + r : rows * PACK + r + 1, :].astype(jnp.float32)
            x = panel_ref[r * PACK : (r + 1) * PACK, :].astype(jnp.float32)
            pieces.extend(widen(x, mask))
        wide = jnp.concatenate(pieces, axis=0)
        restrict_ref[pl.ds(pl.multiple_of(panel * CP * B, LANES), CP * B), :] = wide.T.astype(BF16)


def product_kernel(
    n, code_ref, ghost_ref, left_ref, right_ref, own_ref, coupling_ref, restrict_ref, out_ref, wide, ap
):
    rows = coupling_ref.shape[0]
    span = code_ref.shape[0]
    me = lax.axis_index("row")

    def place(slot, tile, mask):
        even, odd = widen(tile, mask)
        to = pl.multiple_of(slot * B, B)
        wide[pl.ds(to, PACK), :] = even
        wide[pl.ds(pl.multiple_of(to + PACK, PACK), PACK), :] = odd

    def place_slots(first, ref, block):
        for s in range(S2):
            tile = ref[(*block, pl.ds(s * PACK, PACK), slice(None))]
            place(rows + first + s, tile, ref[(*block, pl.ds(S2 * PACK + s, 1), slice(None))])

    for r in range(rows):
        place(r, own_ref[r * PACK : (r + 1) * PACK, :], own_ref[rows * PACK + r : rows * PACK + r + 1, :])
    for j, source in enumerate(alternating(n)):
        place_slots(source * S, ghost_ref, (j,))
    for ref, step in ((left_ref, n - 1), (right_ref, 1)):
        place_slots(lax.rem(me + step, n) * S + S2, ref, ())

    def pair_body(i, carry):
        pair = (2 * i, 2 * i + 1)
        picked = [
            jnp.concatenate(
                [wide[pl.ds(pl.multiple_of(code_ref[k, r] * B, B), B), :] for k in range(span)], axis=0
            )
            for r in pair
        ]
        both = coupling_ref[pl.ds(2 * i, 2), :, : span * B].reshape(2 * B, span * B)
        block = jnp.dot(both, jnp.concatenate(picked, axis=1), preferred_element_type=jnp.float32)
        for h, r in enumerate(pair):
            own = block[h * B : (h + 1) * B, h * LANES : (h + 1) * LANES]
            ap[pl.ds(pl.multiple_of(r * B, B), B), :] = own.astype(BF16)
        return carry

    lax.fori_loop(0, rows // 2, pair_body, 0, unroll=8)
    coarse = jnp.dot(restrict_ref[...], ap[...], preferred_element_type=jnp.float32)
    share = out_ref.shape[0] // n
    for j, target in enumerate(alternating(n)):
        out_ref[j * share : (j + 1) * share, :] = coarse[target * share : (target + 1) * share]


def sum_kernel(parts_ref, out_ref):
    out_ref[...] = jnp.sum(parts_ref[...], axis=0)


def shards(n, col_size, a_tiles, neighbors, send_rows, p_tiles, p_index):
    rows, span = a_tiles.shape[0], a_tiles.shape[1]
    flat = p_tiles[:, 0, :]
    index = p_index.T
    f32 = jnp.float32

    def call(body, out_shape, scratch_shapes, operands, smem, name, flops=10**7):
        return pl.pallas_call(
            body,
            out_shape=out_shape,
            in_specs=[SMEM] * smem + [VMEM] * (len(operands) - smem),
            out_specs=jax.tree.map(lambda _: VMEM, out_shape),
            scratch_shapes=scratch_shapes,
            compiler_params=PARAMS,
            cost_estimate=pl.CostEstimate(flops=flops, bytes_accessed=2**20, transcendentals=0),
            name=name,
        )(*operands)

    def shape(*dims, dtype=BF16):
        return jax.ShapeDtypeStruct(dims, dtype)

    def exchange(x):
        return lax.all_to_all(
            x, "row", split_axis=0, concat_axis=0, tiled=True, axis_index_groups=[alternating(n)]
        )

    def ring(x, step):
        return lax.ppermute(x, "row", [(i, (i + step) % n) for i in range(n)])

    unpacked = pltpu.VMEM((rows, PACK, LANES), f32)
    edge = shape(S2 * PACK + 8, LANES)
    blocks = shape(n, S2 * PACK + 8, LANES)
    out, own, left, right = pl.pallas_call(
        functools.partial(own_kernel, n),
        out_shape=(blocks, shape(rows * PACK + rows, LANES), edge, edge),
        in_specs=[HBM] * 3,
        out_specs=(VMEM,) * 4,
        scratch_shapes=[
            pltpu.SMEM(send_rows.shape, jnp.int32),
            pltpu.SMEM(index.shape, jnp.int32),
            pltpu.VMEM(flat.shape, BF16),
            unpacked,
            pltpu.SemaphoreType.DMA((3,)),
        ],
        compiler_params=pltpu.CompilerParams(vmem_limit_bytes=WHOLE),
        cost_estimate=pl.CostEstimate(flops=10**7, bytes_accessed=2**20, transcendentals=0),
        name="own",
    )(send_rows, index, flat)
    out, own, left, right, a_tiles = lax.optimization_barrier((out, own, left, right, a_tiles))
    ghosts = exchange(out)
    from_right, from_left = ring(left, n - 1), ring(right, 1)
    panels = [own] + [
        lax.ppermute(own, "col", [(i, (i + j) % col_size) for i in range(col_size)])
        for j in range(1, col_size)
    ]
    coupling = call(
        coupling_kernel,
        shape(rows, B, pl.cdiv(span, 2) * LANES),
        [pltpu.VMEM((2, rows, PACK, 2 * LANES), f32)],
        (a_tiles.transpose(1, 0, 2),),
        0,
        "coupling",
        2 * 10**9,
    )
    restrict = call(
        functools.partial(restrict_kernel, rows, col_size),
        shape(col_size * CP * B, rows * B),
        [],
        panels,
        0,
        "restrict",
        2 * 10**8,
    )
    partial = call(
        functools.partial(product_kernel, n),
        shape(col_size * CP * B, CP * B, dtype=f32),
        [pltpu.VMEM(((rows + n * S) * B, LANES), BF16), pltpu.VMEM((rows * B, CP * B), BF16)],
        (neighbors.T, ghosts, from_left, from_right, own, coupling, restrict),
        1,
        "product",
        2 * 10**8,
    )
    parts = exchange(partial.reshape(n, col_size * CP * B // n, CP * B))
    return call(sum_kernel, shape(*parts.shape[1:], dtype=f32), [], (parts,), 0, "sum")


def solution(mesh):
    in_specs = (
        P("row", None, None),
        P("row", None),
        P("row", None),
        P("row", "col", None),
        P("row", "col"),
    )
    out_specs = P("row", "col")
    body = functools.partial(shards, mesh.shape["row"], mesh.shape["col"])
    return jax.shard_map(body, mesh=mesh, in_specs=in_specs, out_specs=out_specs, check_vma=False)
```

```python
import functools

import jax
import jax.numpy as jnp
from jax import lax
from jax.experimental import pallas as pl
from jax.experimental.pallas import tpu as pltpu
from jax.sharding import PartitionSpec as P

B = 64
CP = 2
S = 8
S2 = 4
LANES = 128
PACK = B * B // LANES
BF16 = jnp.bfloat16
VMEM = pl.BlockSpec(memory_space=pltpu.VMEM)
SMEM = pl.BlockSpec(memory_space=pltpu.SMEM)
HBM = pl.BlockSpec(memory_space=pl.ANY)
WHOLE = 60 * 2**20
PARAMS = pltpu.CompilerParams(vmem_limit_bytes=40 * 2**20)


def unpack_rows(flat, scratch):
    for l in range(PACK):
        scratch[:, l, :] = flat[:, l * LANES : (l + 1) * LANES].astype(jnp.float32)


def swap_halves(x):
    return jnp.concatenate([x[:, B:], x[:, :B]], axis=1)


def turn_rows(index_of, scratch, out, base):
    rows = scratch.shape[0]
    for r in range(rows):
        x = scratch[r]
        x = jnp.where(index_of(r) == 0, x, swap_halves(x))
        out[base + r * PACK : base + (r + 1) * PACK, :] = x.astype(BF16)


def mask_row(index, shape):
    lane = lax.broadcasted_iota(jnp.int32, shape, len(shape) - 1)
    return jnp.where((lane >= B) == (index != 0), 1.0, 0.0)


def widen(x, mask):
    return x * mask, swap_halves(x) * mask


def mask_table(index_of, rows):
    sub = lax.broadcasted_iota(jnp.int32, (rows, LANES), 0)
    table = jnp.zeros((rows, LANES), jnp.float32)
    for r in range(rows):
        table = jnp.where(sub == r, mask_row(index_of(r), (rows, LANES)), table)
    return table


def fill(ref, block, table, picks, marks):
    sub = lax.broadcasted_iota(jnp.int32, (marks, LANES), 0)
    mark = jnp.zeros((marks, LANES), jnp.float32)
    for s, (row, index) in enumerate(picks):
        tile = table[pl.ds(pl.multiple_of(row * PACK, PACK), PACK), :]
        ref[(*block, pl.ds(s * PACK, PACK), slice(None))] = tile
        mark = jnp.where(sub == s, mask_row(index, (marks, LANES)), mark)
    ref[(*block, pl.ds(len(picks) * PACK, marks), slice(None))] = mark.astype(BF16)


def alternating(n):
    return [i // 4 + i % 2 * (n // 2) + i // 2 % 2 * (n // 4) for i in range(n)]


def own_kernel(n, send_hbm, index_hbm, flat_hbm, out_ref, own_ref, left_ref, right_ref, *refs):
    send_ref, index_ref, flat_ref, scratch, sems = refs
    rows = flat_ref.shape[0]
    me = lax.axis_index("row")
    pairs = ((flat_hbm, flat_ref), (send_hbm, send_ref), (index_hbm, index_ref))
    copies = [pltpu.make_async_copy(x, y, sems.at[i]) for i, (x, y) in enumerate(pairs)]
    for copy in copies:
        copy.start()
    for copy in copies:
        copy.wait()
    unpack_rows(flat_ref, scratch)
    turn_rows(lambda r: index_ref[0, r], scratch, own_ref, 0)
    own_ref[rows * PACK :, :] = mask_table(lambda r: index_ref[0, r], rows).astype(BF16)

    def look(slot):
        row = send_ref[0, slot]
        return row, index_ref[0, row]

    for j, target in enumerate(alternating(n)):
        fill(out_ref, (j,), own_ref, [look(target * S + s) for s in range(S2)], 8)
    for ref, step in ((left_ref, n - 1), (right_ref, 1)):
        first = lax.rem(me + step, n) * S
        fill(ref, (), own_ref, [look(first + s) for s in range(S2, S)], 8)


def coupling_kernel(a_ref, coupling_ref, scratch):
    span, rows, _ = a_ref.shape
    src = lax.broadcasted_iota(jnp.int32, (2 * LANES, 2 * LANES), 0)
    dst = lax.broadcasted_iota(jnp.int32, (2 * LANES, 2 * LANES), 1)
    odd, block, part = dst // LANES, lax.rem(dst // B, 2), lax.rem(dst, B)
    column = jnp.where(part < B // 2, 2 * part, 2 * part - B + 1)
    order = (src == block * LANES + odd * B + column).astype(BF16)
    for pair in range(pl.cdiv(span, 2)):
        blocks = range(2 * pair, min(2 * pair + 2, span))
        buffer = scratch.at[pair % 2]
        for k in blocks:
            unpack_rows(a_ref.at[k], buffer.at[:, :, pl.ds((k % 2) * LANES, LANES)])
        width = len(blocks) * LANES
        packed = buffer[:, :, :width].reshape(rows * PACK, width).astype(BF16)
        ordered = jnp.dot(packed, order[:width], preferred_element_type=jnp.float32).astype(BF16)
        lanes = pl.ds(pair * LANES, LANES)
        coupling_ref[:, :PACK, lanes] = ordered[:, :LANES].reshape(rows, PACK, LANES)
        coupling_ref[:, PACK:, lanes] = ordered[:, LANES:].reshape(rows, PACK, LANES)


def restrict_kernel(rows, col_size, *refs):
    panel_refs, restrict_ref = refs[:col_size], refs[col_size]
    mine = lax.axis_index("col")
    for j, panel_ref in enumerate(panel_refs):
        panel = lax.rem(mine + col_size - j, col_size)
        pieces = []
        for r in range(rows):
            mask = panel_ref[rows * PACK + r : rows * PACK + r + 1, :].astype(jnp.float32)
            x = panel_ref[r * PACK : (r + 1) * PACK, :].astype(jnp.float32)
            pieces.extend(widen(x, mask))
        wide = jnp.concatenate(pieces, axis=0)
        restrict_ref[pl.ds(pl.multiple_of(panel * CP * B, LANES), CP * B), :] = wide.T.astype(BF16)


def product_kernel(
    n, code_ref, ghost_ref, left_ref, right_ref, own_ref, coupling_ref, restrict_ref, out_ref, wide, ap
):
    rows = coupling_ref.shape[0]
    span = code_ref.shape[0]
    me = lax.axis_index("row")

    def place(slot, tile, mask):
        even, odd = widen(tile, mask)
        to = pl.multiple_of(slot * B, B)
        wide[pl.ds(to, PACK), :] = even
        wide[pl.ds(pl.multiple_of(to + PACK, PACK), PACK), :] = odd

    def place_slots(first, ref, block):
        masks = ref[(*block, pl.ds(S2 * PACK, 8), slice(None))].astype(jnp.float32)
        for s in range(S2):
            tile = ref[(*block, pl.ds(s * PACK, PACK), slice(None))]
            mask = jnp.broadcast_to(masks[s : s + 1], (PACK, LANES)).astype(BF16)
            place(rows + first + s, tile, mask)

    for r in range(rows):
        place(r, own_ref[r * PACK : (r + 1) * PACK, :], own_ref[rows * PACK + r : rows * PACK + r + 1, :])
    for j, source in enumerate(alternating(n)):
        place_slots(source * S, ghost_ref, (j,))
    for ref, step in ((left_ref, n - 1), (right_ref, 1)):
        place_slots(lax.rem(me + step, n) * S + S2, ref, ())

    def pair_body(i, carry):
        pair = (2 * i, 2 * i + 1)
        picked = [
            jnp.concatenate(
                [wide[pl.ds(pl.multiple_of(code_ref[k, r] * B, B), B), :] for k in range(span)], axis=0
            )
            for r in pair
        ]
        both = coupling_ref[pl.ds(2 * i, 2), :, : span * B].reshape(2 * B, span * B)
        block = jnp.dot(both, jnp.concatenate(picked, axis=1), preferred_element_type=jnp.float32)
        for h, r in enumerate(pair):
            own = block[h * B : (h + 1) * B, h * LANES : (h + 1) * LANES]
            ap[pl.ds(pl.multiple_of(r * B, B), B), :] = own.astype(BF16)
        return carry

    lax.fori_loop(0, rows // 2, pair_body, 0, unroll=8)
    coarse = jnp.dot(restrict_ref[...], ap[...], preferred_element_type=jnp.float32)
    share = out_ref.shape[0] // n
    for j, target in enumerate(alternating(n)):
        out_ref[j * share : (j + 1) * share, :] = coarse[target * share : (target + 1) * share]


def shards(n, col_size, a_tiles, neighbors, send_rows, p_tiles, p_index):
    rows, span = a_tiles.shape[0], a_tiles.shape[1]
    flat = p_tiles[:, 0, :]
    index = p_index.T
    f32 = jnp.float32

    def call(body, out_shape, scratch_shapes, operands, smem, name, flops=10**7):
        return pl.pallas_call(
            body,
            out_shape=out_shape,
            in_specs=[SMEM] * smem + [VMEM] * (len(operands) - smem),
            out_specs=jax.tree.map(lambda _: VMEM, out_shape),
            scratch_shapes=scratch_shapes,
            compiler_params=PARAMS,
            cost_estimate=pl.CostEstimate(flops=flops, bytes_accessed=2**20, transcendentals=0),
            name=name,
        )(*operands)

    def shape(*dims, dtype=BF16):
        return jax.ShapeDtypeStruct(dims, dtype)

    def exchange(x):
        return lax.all_to_all(
            x, "row", split_axis=0, concat_axis=0, tiled=True, axis_index_groups=[alternating(n)]
        )

    def ring(x, step):
        return lax.ppermute(x, "row", [(i, (i + step) % n) for i in range(n)])

    unpacked = pltpu.VMEM((rows, PACK, LANES), f32)
    edge = shape(S2 * PACK + 8, LANES)
    blocks = shape(n, S2 * PACK + 8, LANES)
    out, own, left, right = pl.pallas_call(
        functools.partial(own_kernel, n),
        out_shape=(blocks, shape(rows * PACK + rows, LANES), edge, edge),
        in_specs=[HBM] * 3,
        out_specs=(VMEM,) * 4,
        scratch_shapes=[
            pltpu.SMEM(send_rows.shape, jnp.int32),
            pltpu.SMEM(index.shape, jnp.int32),
            pltpu.VMEM(flat.shape, BF16),
            unpacked,
            pltpu.SemaphoreType.DMA((3,)),
        ],
        compiler_params=pltpu.CompilerParams(vmem_limit_bytes=WHOLE),
        cost_estimate=pl.CostEstimate(flops=10**7, bytes_accessed=2**20, transcendentals=0),
        name="own",
    )(send_rows, index, flat)
    out, own, left, right, a_tiles = lax.optimization_barrier((out, own, left, right, a_tiles))
    ghosts = exchange(out)
    from_right, from_left = ring(left, n - 1), ring(right, 1)
    panels = [own] + [
        lax.ppermute(own, "col", [(i, (i + j) % col_size) for i in range(col_size)])
        for j in range(1, col_size)
    ]
    coupling = call(
        coupling_kernel,
        shape(rows, B, pl.cdiv(span, 2) * LANES),
        [pltpu.VMEM((2, rows, PACK, 2 * LANES), f32)],
        (a_tiles.transpose(1, 0, 2),),
        0,
        "coupling",
        2 * 10**9,
    )
    restrict = call(
        functools.partial(restrict_kernel, rows, col_size),
        shape(col_size * CP * B, rows * B),
        [],
        panels,
        0,
        "restrict",
        2 * 10**8,
    )
    partial = call(
        functools.partial(product_kernel, n),
        shape(col_size * CP * B, CP * B, dtype=f32),
        [pltpu.VMEM(((rows + n * S) * B, LANES), BF16), pltpu.VMEM((rows * B, CP * B), BF16)],
        (neighbors.T, ghosts, from_left, from_right, own, coupling, restrict),
        1,
        "product",
        2 * 10**8,
    )
    parts = exchange(partial.reshape(n, col_size * CP * B // n, CP * B))
    return jnp.sum(parts, axis=0)


def solution(mesh):
    in_specs = (
        P("row", None, None),
        P("row", None),
        P("row", None),
        P("row", "col", None),
        P("row", "col"),
    )
    out_specs = P("row", "col")
    body = functools.partial(shards, mesh.shape["row"], mesh.shape["col"])
    return jax.shard_map(body, mesh=mesh, in_specs=in_specs, out_specs=out_specs, check_vma=False)
```

```python
import functools

import jax
import jax.numpy as jnp
from jax import lax
from jax.experimental import pallas as pl
from jax.experimental.pallas import tpu as pltpu
from jax.sharding import PartitionSpec as P

B = 64
CP = 2
S = 8
S2 = 4
LANES = 128
PACK = B * B // LANES
BF16 = jnp.bfloat16
VMEM = pl.BlockSpec(memory_space=pltpu.VMEM)
SMEM = pl.BlockSpec(memory_space=pltpu.SMEM)
HBM = pl.BlockSpec(memory_space=pl.ANY)
WHOLE = 60 * 2**20
PARAMS = pltpu.CompilerParams(vmem_limit_bytes=40 * 2**20)


def unpack_rows(flat, scratch):
    for l in range(PACK):
        scratch[:, l, :] = flat[:, l * LANES : (l + 1) * LANES].astype(jnp.float32)


def swap_halves(x):
    return jnp.concatenate([x[:, B:], x[:, :B]], axis=1)


def turn_rows(index_of, scratch, out, base):
    rows = scratch.shape[0]
    for r in range(rows):
        x = scratch[r]
        x = jnp.where(index_of(r) == 0, x, swap_halves(x))
        out[base + r * PACK : base + (r + 1) * PACK, :] = x.astype(BF16)


def mask_row(index, shape):
    lane = lax.broadcasted_iota(jnp.int32, shape, len(shape) - 1)
    return jnp.where((lane >= B) == (index != 0), 1.0, 0.0)


def widen(x, mask):
    return x * mask, swap_halves(x) * mask


def mask_table(index_of, rows):
    sub = lax.broadcasted_iota(jnp.int32, (rows, LANES), 0)
    table = jnp.zeros((rows, LANES), jnp.float32)
    for r in range(rows):
        table = jnp.where(sub == r, mask_row(index_of(r), (rows, LANES)), table)
    return table


def fill(ref, block, table, picks, marks):
    sub = lax.broadcasted_iota(jnp.int32, (marks, LANES), 0)
    mark = jnp.zeros((marks, LANES), jnp.float32)
    for s, (row, index) in enumerate(picks):
        tile = table[pl.ds(pl.multiple_of(row * PACK, PACK), PACK), :]
        ref[(*block, pl.ds(s * PACK, PACK), slice(None))] = tile
        mark = jnp.where(sub == s, mask_row(index, (marks, LANES)), mark)
    ref[(*block, pl.ds(len(picks) * PACK, marks), slice(None))] = mark.astype(BF16)


def alternating(n):
    return [i // 4 + i % 2 * (n // 2) + i // 2 % 2 * (n // 4) for i in range(n)]


def own_kernel(n, send_hbm, index_hbm, flat_hbm, out_ref, own_ref, left_ref, right_ref, *refs):
    send_ref, index_ref, flat_ref, scratch, sems = refs
    rows = flat_ref.shape[0]
    me = lax.axis_index("row")
    pairs = ((flat_hbm, flat_ref), (send_hbm, send_ref), (index_hbm, index_ref))
    copies = [pltpu.make_async_copy(x, y, sems.at[i]) for i, (x, y) in enumerate(pairs)]
    for copy in copies:
        copy.start()
    copies[0].wait()
    unpack_rows(flat_ref, scratch)
    copies[1].wait()
    copies[2].wait()
    turn_rows(lambda r: index_ref[0, r], scratch, own_ref, 0)
    own_ref[rows * PACK :, :] = mask_table(lambda r: index_ref[0, r], rows).astype(BF16)

    def look(slot):
        row = send_ref[0, slot]
        return row, index_ref[0, row]

    for j, target in enumerate(alternating(n)):
        fill(out_ref, (j,), own_ref, [look(target * S + s) for s in range(S2)], 8)
    for ref, step in ((left_ref, n - 1), (right_ref, 1)):
        first = lax.rem(me + step, n) * S
        fill(ref, (), own_ref, [look(first + s) for s in range(S2, S)], 8)


def coupling_kernel(a_ref, coupling_ref, scratch):
    span, rows, _ = a_ref.shape
    src = lax.broadcasted_iota(jnp.int32, (2 * LANES, 2 * LANES), 0)
    dst = lax.broadcasted_iota(jnp.int32, (2 * LANES, 2 * LANES), 1)
    odd, block, part = dst // LANES, lax.rem(dst // B, 2), lax.rem(dst, B)
    column = jnp.where(part < B // 2, 2 * part, 2 * part - B + 1)
    order = (src == block * LANES + odd * B + column).astype(BF16)
    for pair in range(pl.cdiv(span, 2)):
        blocks = range(2 * pair, min(2 * pair + 2, span))
        buffer = scratch.at[pair % 2]
        for k in blocks:
            unpack_rows(a_ref.at[k], buffer.at[:, :, pl.ds((k % 2) * LANES, LANES)])
        width = len(blocks) * LANES
        packed = buffer[:, :, :width].reshape(rows * PACK, width).astype(BF16)
        ordered = jnp.dot(packed, order[:width], preferred_element_type=jnp.float32).astype(BF16)
        lanes = pl.ds(pair * LANES, LANES)
        coupling_ref[:, :PACK, lanes] = ordered[:, :LANES].reshape(rows, PACK, LANES)
        coupling_ref[:, PACK:, lanes] = ordered[:, LANES:].reshape(rows, PACK, LANES)


def restrict_kernel(rows, col_size, *refs):
    panel_refs, restrict_ref = refs[:col_size], refs[col_size]
    mine = lax.axis_index("col")
    for j, panel_ref in enumerate(panel_refs):
        panel = lax.rem(mine + col_size - j, col_size)
        pieces = []
        for r in range(rows):
            mask = panel_ref[rows * PACK + r : rows * PACK + r + 1, :].astype(jnp.float32)
            x = panel_ref[r * PACK : (r + 1) * PACK, :].astype(jnp.float32)
            pieces.extend(widen(x, mask))
        wide = jnp.concatenate(pieces, axis=0)
        restrict_ref[pl.ds(pl.multiple_of(panel * CP * B, LANES), CP * B), :] = wide.T.astype(BF16)


def product_kernel(
    n, code_ref, ghost_ref, left_ref, right_ref, own_ref, coupling_ref, restrict_ref, out_ref, wide, ap
):
    rows = coupling_ref.shape[0]
    span = code_ref.shape[0]
    me = lax.axis_index("row")

    def place(slot, tile, mask):
        even, odd = widen(tile, mask)
        to = pl.multiple_of(slot * B, B)
        wide[pl.ds(to, PACK), :] = even
        wide[pl.ds(pl.multiple_of(to + PACK, PACK), PACK), :] = odd

    def place_slots(first, ref, block):
        for s in range(S2):
            tile = ref[(*block, pl.ds(s * PACK, PACK), slice(None))]
            place(rows + first + s, tile, ref[(*block, pl.ds(S2 * PACK + s, 1), slice(None))])

    for r in range(rows):
        place(r, own_ref[r * PACK : (r + 1) * PACK, :], own_ref[rows * PACK + r : rows * PACK + r + 1, :])
    for j, source in enumerate(alternating(n)):
        place_slots(source * S, ghost_ref, (j,))
    for ref, step in ((left_ref, n - 1), (right_ref, 1)):
        place_slots(lax.rem(me + step, n) * S + S2, ref, ())

    def pair_body(i, carry):
        pair = (2 * i, 2 * i + 1)
        picked = [
            jnp.concatenate(
                [wide[pl.ds(pl.multiple_of(code_ref[k, r] * B, B), B), :] for k in range(span)], axis=0
            )
            for r in pair
        ]
        both = coupling_ref[pl.ds(2 * i, 2), :, : span * B].reshape(2 * B, span * B)
        block = jnp.dot(both, jnp.concatenate(picked, axis=1), preferred_element_type=jnp.float32)
        for h, r in enumerate(pair):
            own = block[h * B : (h + 1) * B, h * LANES : (h + 1) * LANES]
            ap[pl.ds(pl.multiple_of(r * B, B), B), :] = own.astype(BF16)
        return carry

    lax.fori_loop(0, rows // 2, pair_body, 0, unroll=8)
    coarse = jnp.dot(restrict_ref[...], ap[...], preferred_element_type=jnp.float32)
    share = out_ref.shape[0] // n
    for j, target in enumerate(alternating(n)):
        out_ref[j * share : (j + 1) * share, :] = coarse[target * share : (target + 1) * share]


def shards(n, col_size, a_tiles, neighbors, send_rows, p_tiles, p_index):
    rows, span = a_tiles.shape[0], a_tiles.shape[1]
    flat = p_tiles[:, 0, :]
    index = p_index.T
    f32 = jnp.float32

    def call(body, out_shape, scratch_shapes, operands, smem, name, flops=10**7):
        return pl.pallas_call(
            body,
            out_shape=out_shape,
            in_specs=[SMEM] * smem + [VMEM] * (len(operands) - smem),
            out_specs=jax.tree.map(lambda _: VMEM, out_shape),
            scratch_shapes=scratch_shapes,
            compiler_params=PARAMS,
            cost_estimate=pl.CostEstimate(flops=flops, bytes_accessed=2**20, transcendentals=0),
            name=name,
        )(*operands)

    def shape(*dims, dtype=BF16):
        return jax.ShapeDtypeStruct(dims, dtype)

    def exchange(x):
        return lax.all_to_all(
            x, "row", split_axis=0, concat_axis=0, tiled=True, axis_index_groups=[alternating(n)]
        )

    def ring(x, step):
        return lax.ppermute(x, "row", [(i, (i + step) % n) for i in range(n)])

    unpacked = pltpu.VMEM((rows, PACK, LANES), f32)
    edge = shape(S2 * PACK + 8, LANES)
    blocks = shape(n, S2 * PACK + 8, LANES)
    out, own, left, right = pl.pallas_call(
        functools.partial(own_kernel, n),
        out_shape=(blocks, shape(rows * PACK + rows, LANES), edge, edge),
        in_specs=[HBM] * 3,
        out_specs=(VMEM,) * 4,
        scratch_shapes=[
            pltpu.SMEM(send_rows.shape, jnp.int32),
            pltpu.SMEM(index.shape, jnp.int32),
            pltpu.VMEM(flat.shape, BF16),
            unpacked,
            pltpu.SemaphoreType.DMA((3,)),
        ],
        compiler_params=pltpu.CompilerParams(vmem_limit_bytes=WHOLE),
        cost_estimate=pl.CostEstimate(flops=10**7, bytes_accessed=2**20, transcendentals=0),
        name="own",
    )(send_rows, index, flat)
    out, own, left, right, a_tiles = lax.optimization_barrier((out, own, left, right, a_tiles))
    ghosts = exchange(out)
    from_right, from_left = ring(left, n - 1), ring(right, 1)
    panels = [own] + [
        lax.ppermute(own, "col", [(i, (i + j) % col_size) for i in range(col_size)])
        for j in range(1, col_size)
    ]
    coupling = call(
        coupling_kernel,
        shape(rows, B, pl.cdiv(span, 2) * LANES),
        [pltpu.VMEM((2, rows, PACK, 2 * LANES), f32)],
        (a_tiles.transpose(1, 0, 2),),
        0,
        "coupling",
        2 * 10**9,
    )
    restrict = call(
        functools.partial(restrict_kernel, rows, col_size),
        shape(col_size * CP * B, rows * B),
        [],
        panels,
        0,
        "restrict",
        2 * 10**8,
    )
    partial = call(
        functools.partial(product_kernel, n),
        shape(col_size * CP * B, CP * B, dtype=f32),
        [pltpu.VMEM(((rows + n * S) * B, LANES), BF16), pltpu.VMEM((rows * B, CP * B), BF16)],
        (neighbors.T, ghosts, from_left, from_right, own, coupling, restrict),
        1,
        "product",
        2 * 10**8,
    )
    parts = exchange(partial.reshape(n, col_size * CP * B // n, CP * B))
    return jnp.sum(parts, axis=0)


def solution(mesh):
    in_specs = (
        P("row", None, None),
        P("row", None),
        P("row", None),
        P("row", "col", None),
        P("row", "col"),
    )
    out_specs = P("row", "col")
    body = functools.partial(shards, mesh.shape["row"], mesh.shape["col"])
    return jax.shard_map(body, mesh=mesh, in_specs=in_specs, out_specs=out_specs, check_vma=False)
```
